128 devices in a mesh: lon: 16 (over y, z_hi, core), lat: 8 (over z_lo, x).
Axes of the slice: x: 4, y: 4, z: 4 (z_hi: 2, z_lo: 2; z = z_hi * 2 + z_lo), core: 2. Of those that a mesh axis runs over, the one named last changes fastest.
Arguments:
- background: float32 [69, 128, 2048], P(None, 'lon', 'lat'), may hold values from -6 to 6
- encoder_weight: bfloat16 [128, 69], replicated, may hold values from -0.75 to 0.75
- convolution_weight: bfloat16 [4, 9, 128, 128], replicated, may hold values from -0.1875 to 0.1875
- decoder_weight: bfloat16 [69, 128], replicated, may hold values from -0.5 to 0.5
- dilations: int32 [4], replicated, may hold values from 1 to 4, as said below
- obs_values: float32 [69, 65536], P(None, ('lon', 'lat')), may hold values from -6 to 6
- obs_prec: float32 [65536], P(('lon', 'lat')), may hold values from 0.25 to 4
- obs_frac: float32 [2, 65536], P(None, ('lon', 'lat')), may hold values from 0 to 1
- obs_dest: int32 [65536, 1], P(('lon', 'lat')), may hold values from 0 to 127; in each aligned block of 512 rows (0 to 511, 512 to 1023, ...) at most 8 rows name the same one
- obs_cell: int32 [65536], P(('lon', 'lat')), may hold values from 0 to 1784
- obs_count: int32 [128], P(('lon', 'lat')), may hold values from 256 to 512, as said below
Outputs:
- analysis: float32 [69, 128, 2048], P(None, 'lon', 'lat')
- innovations: float32 [69, 65536], P(None, ('lon', 'lat'))
The draws below stay inside these ranges and needn't reach their ends.
Inputs may be any that keep to these rules, and one draw needn't show every extreme that they name: `dilations`: every layer's dilation lies in 1 to 4, and some layer has dilation 4. `obs_dest`: devices are numbered 8 * lon index + lat index. Among the 512 rows of one device no owner is named more than 8 times, a bound that some block reaches. `obs_cell`: the code c places the lower stencil corner at local longitude c // 255 and local latitude c % (255) of the owner's block, so all four stencil cells lie in that block. `obs_count`: some device has all 512 rows live.
All inputs are finite; a program needn't handle non-finite values.
Results may differ from the reference program's by a relative error of at most 0.023.
Values may be sent and summed in bfloat16 or wider, within the bound.
No kernel may reach another device: no remote copies, remote signals or barrier semaphores. Data moves between devices by JAX's collectives and lax.ppermute only.
A program may use at most 128 MiB of HBM per device.

```python
import math
import jax
import jax.numpy as jnp
import numpy as np
from jax import lax

VARS = 69
C = 128
DMAX = 4
LAYERS = 4
ITERS = 2
CLON = 8
CLAT = 256
OBS_DEV = 512
NLON = 128
NLAT = 2048
NOBS = 65536
N_LAT = 8
DEVICES = 128


def draw_dilations(key, part):
    values = jax.random.randint(jax.random.fold_in(key, 11), (LAYERS,), 1, DMAX + 1).astype(jnp.int32)
    position = jax.random.randint(jax.random.fold_in(key, 12), (), 0, LAYERS)
    return values.at[position].set(DMAX)


def draw_obs_count(key, part):
    values = jax.random.randint(jax.random.fold_in(key, 21), (DEVICES,), OBS_DEV // 2, OBS_DEV + 1).astype(jnp.int32)
    position = jax.random.randint(jax.random.fold_in(key, 22), (), 0, DEVICES)
    return values.at[position].set(OBS_DEV)


def place_ends(array, key, smallest, top_value):
    longest = array.shape.index(max(array.shape))
    spots = []
    for shift in (0, 1):
        where = [jax.random.randint(jax.random.fold_in(key, axis), (), 0, length) for axis, length in enumerate(array.shape)]
        where[longest] = (where[longest] + shift) % array.shape[longest]
        spots.append(tuple(where))
    return array.at[spots[0]].set(smallest).at[spots[1]].set(top_value)


def level_of(key, shape, pieces, smallest, high):
    def one(dim, shards_of):
        draws = jax.random.uniform(jax.random.fold_in(jax.random.fold_in(key, 6), dim), (shards_of,), jnp.float32, smallest / len(pieces), high / len(pieces))
        return jnp.repeat(jnp.exp(draws), shape[dim] // shards_of).reshape((-1,) + (1,) * (len(shape) - dim - 1))

    gain = one(*pieces[0])
    for cut in pieces[1:]:
        gain = gain * one(*cut)
    return gain


def routed_block(rng, own, number, rows, count, top, bound, lean):
    order = jax.random.permutation(rng, count)
    crowded, common = load_shares(count, rows * top, bound, lean, True), load_shares(count, rows * top, bound, lean, False)
    places = jnp.arange(count)

    def named(sizes, turn):
        used = int((sizes > 0).sum())
        fixed = max(1, used // 4)
        moved = fixed + (places - fixed + turn * (used - fixed)) % max(1, count - fixed)
        return jnp.zeros((count,), jnp.int32).at[order[jnp.where(places < fixed, places, moved)]].set(jnp.asarray(sizes, jnp.int32))

    sizes = jnp.where(number % 4 == 0, named(crowded, number // 4), named(common, number - number // 4 - 1))
    mixed = jax.random.permutation(jax.random.fold_in(own, 3), count)
    giver, receiver = mixed[0:count // 2 * 2:2], mixed[1:count // 2 * 2:2]
    slack = jnp.minimum(sizes[giver] - 1, bound - sizes[receiver]) // 2
    slack = jnp.where((giver == order[0]) | (receiver == order[0]) | (sizes[receiver] == 0), 0, jnp.maximum(slack, 0))
    moved = jax.random.randint(jax.random.fold_in(own, 4), (count // 2,), 0, 1 << 20) % (slack + 1)
    sizes = sizes.at[giver].add(-moved).at[receiver].add(moved)
    members = jnp.searchsorted(jnp.cumsum(sizes), jnp.arange(rows * top), side="right").astype(jnp.int32)
    listing = members.reshape(top, rows).T
    listing = listing[jax.random.permutation(jax.random.fold_in(own, 1), rows)]
    turn = jax.random.randint(jax.random.fold_in(own, 2), (rows, 1), 0, top)
    return jnp.take_along_axis(listing, (jnp.arange(top)[None, :] + turn) % top, axis=1)


def load_shares(amount, total, limit, slope, full):
    weights = [(1 << 20) // math.isqrt(rank ** slope) + 1 for rank in range(1, amount + 1)]
    largest = limit if full else min(limit, max(-(-total // amount), total * weights[0] // sum(weights)))
    least = 1 if total - largest >= amount - 1 else 0
    given, surplus = [largest] + [least] * (amount - 1), total - largest - least * (amount - 1)
    while surplus > 0:
        candidates = [i for i in range(1, amount) if given[i] < largest] or [i for i in range(1, amount) if given[i] < limit]
        pool, remaining = sum([weights[i] for i in candidates]), surplus
        for i in candidates:
            more = min(limit - given[i], max(1, remaining * weights[i] // pool), surplus)
            given[i] = given[i] + more
            surplus = surplus - more
    return np.array(given)


def normal_values(key, shape, scale, reach, split=(), kind=jnp.bfloat16):
    gain = level_of(key, shape, split, -0.22, 0.18) if split else 1.0
    result = jax.random.normal(key, shape, jnp.float32) * scale * gain
    return jnp.minimum(jnp.maximum(result, -reach), reach).astype(kind)


def setup_inputs(seed: int = 0) -> dict:
    splits = jax.random.split(jax.random.key(seed), 12)
    background = normal_values(splits[0], (VARS, NLON, NLAT), 1.0, 6.0, ((1, 16), (2, 8)), jnp.float32)
    encoder_weight = normal_values(splits[1], (C, VARS), VARS ** -0.5, 0.75)
    convolution_weight = normal_values(splits[2], (LAYERS, 9, C, C), (9 * C) ** -0.5, 0.1875)
    decoder_weight = normal_values(splits[3], (VARS, C), C ** -0.5, 0.5)
    dilations = draw_dilations(jax.random.fold_in(splits[11], 71), 0)
    obs_values = normal_values(splits[5], (VARS, NOBS), 1.0, 6.0, ((1, 128),), jnp.float32)
    obs_prec = jnp.clip(jnp.exp(math.log(4.0) - 2.7725887 * jax.random.uniform(splits[6], (NOBS,), jnp.float32) ** level_of(splits[6], (NOBS,), ((0, 128),), -0.2, 0.2)), 0.25, 4.0)
    obs_frac = jnp.clip(1.0 * jax.random.uniform(splits[7], (2, NOBS), jnp.float32) ** level_of(splits[7], (2, NOBS), ((1, 128),), -0.2, 0.2), 0.0, 1.0)
    obs_dest_keys = jax.random.split(jax.random.fold_in(splits[8], 1), NOBS // OBS_DEV)
    obs_dest_turns = jax.random.permutation(jax.random.fold_in(splits[8], 3), NOBS // OBS_DEV)
    obs_dest = jax.vmap(lambda own, number: routed_block(jax.random.fold_in(splits[8], 2), own, number, OBS_DEV, DEVICES, 1, 2 * OBS_DEV // DEVICES, 2))(obs_dest_keys, obs_dest_turns).reshape((NOBS, 1))
    obs_cell = place_ends(jax.random.randint(splits[9], (NOBS,), 0, (CLON - 1) * (CLAT - 1)), jax.random.fold_in(splits[9], 1), 0, ((CLON - 1) * (CLAT - 1)) - 1).astype(jnp.int32)
    obs_count = draw_obs_count(jax.random.fold_in(splits[11], 71), 0)
    return {"background": background, "encoder_weight": encoder_weight, "convolution_weight": convolution_weight, "decoder_weight": decoder_weight, "dilations": dilations, "obs_values": obs_values, "obs_prec": obs_prec, "obs_frac": obs_frac, "obs_dest": obs_dest, "obs_cell": obs_cell, "obs_count": obs_count}


step_size = 0.25


def shifted(field, move_lon, move_lat):
    rolled = jnp.roll(field, -move_lon, axis=1)
    padded = jnp.pad(rolled, ((0, 0), (0, 0), (DMAX, DMAX)))
    return lax.dynamic_slice_in_dim(padded, DMAX + move_lat, NLAT, 2)


def convolve(activity, kernels, dilation, backward):
    summed = jnp.zeros(activity.shape, jnp.float32)
    source = activity.astype(jnp.float32)
    for step_lon in (-1, 0, 1):
        for step_lat in (-1, 0, 1):
            tap_index = 3 * (step_lon + 1) + (step_lat + 1)
            kernel = kernels[tap_index].astype(jnp.float32)
            if backward:
                window = shifted(source, -step_lon * dilation, -step_lat * dilation)
                summed = summed + jnp.einsum("oc,ohw->chw", kernel, window)
            else:
                window = shifted(source, step_lon * dilation, step_lat * dilation)
                summed = summed + jnp.einsum("oc,chw->ohw", kernel, window)
    return summed


def reference(background, encoder_weight, convolution_weight, decoder_weight, dilations, obs_values, obs_prec, obs_frac, obs_dest, obs_cell, obs_count):
    row_index = jnp.arange(NOBS, dtype=jnp.int32)
    holder_of = row_index // OBS_DEV
    live = (row_index % OBS_DEV < obs_count[holder_of]).astype(jnp.float32)
    target = obs_dest[:, 0]
    base_lon = (target // N_LAT) * CLON + obs_cell // (CLAT - 1)
    base_lat = (target % N_LAT) * CLAT + obs_cell % (CLAT - 1)
    frac_lon = obs_frac[0]
    frac_lat = obs_frac[1]
    corners = ((base_lon, base_lat), (base_lon + 1, base_lat), (base_lon, base_lat + 1), (base_lon + 1, base_lat + 1))
    weights = ((1.0 - frac_lon) * (1.0 - frac_lat), frac_lon * (1.0 - frac_lat), (1.0 - frac_lon) * frac_lat, frac_lon * frac_lat)
    field_to_latent_map = encoder_weight.astype(jnp.float32)
    latent_to_field_map = decoder_weight.astype(jnp.float32)
    current_field = background
    innovation = jnp.zeros_like(obs_values)
    for iteration in range(ITERS):
        latent_width = jnp.einsum("cv,vhw->chw", field_to_latent_map, current_field.astype(jnp.bfloat16).astype(jnp.float32))
        field_history = []
        for layer_index in range(LAYERS):
            field_history.append(latent_width)
            activity = jnp.tanh(latent_width).astype(jnp.bfloat16)
            latent_width = latent_width + convolve(activity, convolution_weight[layer_index], dilations[layer_index], False)
        predicted_field = current_field + jnp.einsum("pf,fms->pms", latent_to_field_map, latent_width.astype(jnp.bfloat16).astype(jnp.float32))
        counterpart_of_measurement = jnp.zeros_like(obs_values)
        for lower_left_gridnode, scaling_coefficient in zip(corners, weights):
            counterpart_of_measurement = counterpart_of_measurement + scaling_coefficient[None, :] * predicted_field[:, lower_left_gridnode[0], lower_left_gridnode[1]]
        innovation = live[None, :] * (counterpart_of_measurement - obs_values)
        scaled_departure = obs_prec[None, :] * innovation
        predicted_sensitivity = jnp.zeros_like(predicted_field)
        for lower_left_gridnode, scaling_coefficient in zip(corners, weights):
            predicted_sensitivity = predicted_sensitivity.at[:, lower_left_gridnode[0], lower_left_gridnode[1]].add(scaling_coefficient[None, :] * scaled_departure)
        reverse_sweep_carry = jnp.einsum("hi,heb->ieb", latent_to_field_map, predicted_sensitivity.astype(jnp.bfloat16).astype(jnp.float32))
        for layer_index in reversed(range(LAYERS)):
            adjoint = convolve(reverse_sweep_carry.astype(jnp.bfloat16), convolution_weight[layer_index], dilations[layer_index], True)
            squashed = jnp.tanh(field_history[layer_index])
            reverse_sweep_carry = reverse_sweep_carry + (1.0 - squashed * squashed) * adjoint
        field_sensitivity = predicted_sensitivity + jnp.einsum("bk,bhn->khn", field_to_latent_map, reverse_sweep_carry.astype(jnp.bfloat16).astype(jnp.float32))
        current_field = current_field - step_size * ((current_field - background) + field_sensitivity)
    return current_field, innovation
```

```python
import functools

import jax
import jax.numpy as jnp
from jax import lax
from jax.experimental import pallas as pl
from jax.experimental.pallas import tpu as pltpu
from jax.sharding import PartitionSpec as P

AXES = ("lon", "lat")
BF = jnp.bfloat16
F32 = jnp.float32
V = 72
OFF = 8
ROWS = 88
R = 8
STEP = 0.25
VMEM = 60 * 1024 * 1024


def snake(s, lat):
    return s if lat % 2 == 0 else 3 - s


def device(lon, lat):
    return 8 * lon + lat


def worker(y, p):
    lat, k = p // 4, p % 4
    return device(4 * y + snake(k, lat), lat)


LON_UP = [(worker(y, p), worker((y + 1) % 4, p)) for y in range(4) for p in range(32)]
LON_DOWN = [(b, a) for a, b in LON_UP]
LAT_UP = [(worker(y, p), worker(y, p + 1)) for y in range(4) for p in range(31)]
LAT_DOWN = [(b, a) for a, b in LAT_UP]
BAND_UP = [(device(n, l), device(n, l + 1)) for n in range(16) for l in range(7)]
BAND_DOWN = [(b, a) for a, b in BAND_UP]
GROUPS_32 = [[device(4 * y + s, l) for y in range(4) for l in range(8)] for s in range(4)]
GROUPS_4 = [[device(4 * y + s, l) for s in range(4)] for y in range(4) for l in range(8)]


def family(m):
    pairs = []
    for y in range(4):
        for s in range(4):
            to = y if m < 4 else (y + (1 if s >= 2 else -1)) % 4
            for l in range(8):
                pairs.append((device(4 * y + s, l), device(4 * to + (s + m) % 4, l)))
    return pairs


def nt(a, b):
    return lax.dot_general(a, b, (((1,), (1,)), ((), ())), preferred_element_type=F32)


def tn(a, b):
    return lax.dot_general(a, b, (((0,), (0,)), ((), ())), preferred_element_type=F32)


def nn(a, b):
    return jnp.dot(a, b, preferred_element_type=F32)


def compact_kernel(scal, pay, comp, posx, count, total):
    k64 = scal[6].astype(F32)
    mine, own = [], []
    for part in range(4):
        ctrl = pay[part].astype(F32)[72:80]
        local = ctrl[7:8] - k64
        live = ctrl[0:1] > 0.0
        mine.append(jnp.where(live & (local >= -1.0) & (local <= 63.0), 1.0, 0.0))
        own.append(jnp.where(live & (local >= 0.0) & (local <= 63.0), 1.0, 0.0))
    mine = jnp.concatenate([m[:, 128 * c : 128 * c + 128] for m in mine for c in range(8)], axis=0)
    own = jnp.concatenate([m[:, 128 * c : 128 * c + 128] for m in own for c in range(8)], axis=0)
    row = lax.broadcasted_iota(jnp.int32, (128, 128), 0)
    col = lax.broadcasted_iota(jnp.int32, (128, 128), 1)
    before = nn(mine.astype(BF), jnp.where(row < col, 1.0, 0.0).astype(BF))
    sums = nn(mine.astype(BF), jnp.ones((128, 128), BF))
    row4 = lax.broadcasted_iota(jnp.int32, (32, 32), 0)
    col4 = lax.broadcasted_iota(jnp.int32, (32, 32), 1)
    offset = nn(jnp.where(col4 < row4, 1.0, 0.0).astype(BF), sums.astype(BF))
    place = before + offset
    posx[...] = jnp.where(own > 0.0, place, -1.0)
    total[...] = jnp.where(mine > 0.0, place, -1.0)
    number = jnp.sum(mine).astype(jnp.int32)
    count[0] = number
    comp[...] = jnp.zeros_like(comp)
    index = lax.broadcasted_iota(jnp.int32, (256, 128), 0).astype(F32)

    @pl.loop(0, (number + 255) // 256)
    def _(tile):
        ids = index + (tile * 256).astype(F32)
        out = jnp.zeros((80, 256), F32)
        for c in range(0, 32, 2):
            picks = jnp.concatenate(
                [jnp.where(ids == total[c + h : c + h + 1, :], 1.0, 0.0).astype(BF) for h in (0, 1)], axis=1
            )
            out = out + nt(pay[c // 8, :, 128 * (c % 8) : 128 * (c % 8) + 256], picks)
        comp[:, pl.ds(pl.multiple_of(tile * 256, 256), 256)] = out.astype(BF)


def expand_kernel(count, posx, found, out, total):
    index = lax.broadcasted_iota(jnp.int32, (256, 128), 0).astype(F32)
    total[...] = jnp.zeros_like(total)

    @pl.loop(0, (count[0] + 255) // 256)
    def _(tile):
        ids = index + (tile * 256).astype(F32)
        rows = found[:, pl.ds(pl.multiple_of(tile * 256, 256), 256)]
        for c in range(32):
            picks = jnp.where(ids == posx[c : c + 1, :], 1.0, 0.0).astype(BF)
            total[c // 8, :, 128 * (c % 8) : 128 * (c % 8) + 128] += nn(rows, picks)

    out[...] = total[...].astype(BF)


def iterate(second, *refs):
    scal, count = refs[0:2]
    chunks = refs[2:10]
    enc_t, enc_eye, dec_eye, dec_n, eye, wf, wb, comp = refs[10:18]
    refs = refs[18:]
    if second:
        tots, from_prev, from_next = refs[0:2], refs[2], refs[3]
        outs, found = refs[4:12], refs[12]
        refs = refs[13:]
    else:
        outs = refs[0:2]
        refs = refs[2:]
    st, h, act, slope, bk, fct, wobs, g, ga = refs

    for f in range(8):
        base = 8 * scal[8 + f]
        for r in range(8):
            st[base + r] = tn(chunks[f][r], eye[...])
    if second:
        for half in range(2):
            tot = tots[half]
            for c in range(2):
                rows = pl.ds(32 * half + 16 * c, 16)
                lanes = 1024 * half + 512 * c
                for sec in range(3):
                    add = tot[:, 1024 * sec + 512 * c : 1024 * sec + 512 * c + 512].astype(F32)
                    if sec == 0:
                        add = add + from_prev[:, lanes : lanes + 512].astype(F32)
                    if sec == 2:
                        add = add + from_next[:, lanes : lanes + 512].astype(F32)
                    add = tn(add.astype(BF), eye[...]).reshape(16, 32, 128)
                    st[rows, 16 + 32 * sec : 48 + 32 * sec, :] -= STEP * add
                    if half + c == 1:
                        ga[pl.ds(16 * c_own(half, c), 16), 32 * sec : 32 * sec + 32, :] = 0.75 * add
            low = tn(from_prev[:, 2048 + 128 * half : 2176 + 128 * half], eye[...])
            high = tn(from_next[:, 2048 + 128 * half : 2176 + 128 * half], eye[...])
            for i in range(32):
                st[32 * half + i, 15:16, :] -= STEP * low[32 + i : 33 + i]
                st[32 * half + i, 112:113, :] -= STEP * high[i : i + 1]

    @pl.loop(0, 8)
    def _(c):
        x = st[pl.ds(8 * c, 8)].reshape(1024, 128).astype(BF)
        h[pl.ds(8 * c + OFF, 8)] = nn(x, enc_t[...]).reshape(8, 128, 128)

    e = lax.broadcasted_iota(jnp.int32, (112, 128), 0) + 8
    mask = jnp.where((e >= scal[4]) & (e < scal[5]), 1.0, 0.0)

    @pl.loop(0, 4)
    def _(l):
        d, reach = scal[l], scal[16 + l]
        first = 16 - reach - d + OFF

        @pl.loop(0, 16 + reach + d)
        def _(q):
            for u in range(2):
                i = first + 2 * q + u
                t = jnp.tanh(h[i, 8:120, :])
                slope[l, i] = ((1.0 - t * t) * mask)[8:104].astype(BF)
                t = t * mask
                act[i, :, 0:128] = pltpu.roll(t, d, 0)[8:104].astype(BF)
                act[i, :, 128:256] = t[8:104].astype(BF)
                act[i, :, 256:384] = pltpu.roll(t, 112 - d, 0)[8:104].astype(BF)

        for u in range(R):
            slope[l, 48 + reach + d + OFF + u] = jnp.zeros((96, 128), BF)

        @pl.loop(0, (32 + 2 * reach + R - 1) // R)
        def _(c):
            i = 16 - reach + OFF + R * c
            total = nn(act[pl.ds(i - d, R)].reshape(R * 96, 384), wf[l, 0:384])
            total = total + nn(act[pl.ds(i, R)].reshape(R * 96, 384), wf[l, 384:768])
            total = total + nn(act[pl.ds(i + d, R)].reshape(R * 96, 384), wf[l, 768:1152])
            h[pl.ds(i, R), 16:112, :] += total.reshape(R, 96, 128)

    for c in range(4):
        a = h[16 + OFF + 8 * c : 24 + OFF + 8 * c, 16:112, :].reshape(768, 128).astype(BF)
        b = st[16 + 8 * c : 24 + 8 * c, 16:112, :].reshape(768, 128).astype(BF)
        fct[:, 768 * c : 768 * c + 768] = nt(dec_eye[...], jnp.concatenate([a, b], axis=1)).astype(BF)

    g[...] = jnp.zeros_like(g)
    k64 = scal[6].astype(F32)
    lon_of = lax.broadcasted_iota(jnp.int32, (32, 256), 0).astype(F32)
    lat_of = lax.broadcasted_iota(jnp.int32, (96, 256), 0).astype(F32) - 16.0

    @pl.loop(0, (count[0] + 255) // 256)
    def _(tile):
        lanes = pl.ds(pl.multiple_of(tile * 256, 256), 256)
        pay = comp[:, lanes].astype(F32)
        prec = pay[72:73] + pay[73:74]
        fu = pay[74:75] + pay[75:76]
        fv = pay[76:77] + pay[77:78]
        li, lj = pay[78:79], pay[79:80] - k64
        wa = jnp.where(lon_of == li, 1.0 - fu, 0.0) + jnp.where(lon_of == li + 1.0, fu, 0.0)
        wl = (jnp.where(lat_of == lj, 1.0 - fv, 0.0) + jnp.where(lat_of == lj + 1.0, fv, 0.0)).astype(BF)
        wa = wa.astype(BF)
        for i in range(32):
            wobs[96 * i : 96 * i + 96, :] = wa[i : i + 1] * wl
        eq = nn(fct[...], wobs[...])
        if second:
            found[:, lanes] = eq.astype(BF)
        wt = (prec * (eq - pay[0:72])).astype(BF)
        wt = jnp.concatenate([wt, jnp.zeros((56, 256), BF)], axis=0)
        for c in range(4):
            g[pl.ds(8 * c, 8)] += nt(wobs[768 * c : 768 * c + 768, :], wt).reshape(8, 96, 128)

    g[:, 0:16, :] = jnp.zeros((32, 16, 128), F32)
    g[:, 80:96, :] = jnp.zeros((32, 16, 128), F32)

    bk[...] = jnp.zeros_like(bk)
    act[0:24] = jnp.zeros((24, 96, 384), BF)
    act[56:88] = jnp.zeros((32, 96, 384), BF)
    for c in range(4):
        x = g[8 * c : 8 * c + 8].reshape(768, 128).astype(BF)
        bk[16 + OFF + 8 * c : 24 + OFF + 8 * c] = nn(x, dec_n[...]).reshape(8, 96, 128)

    @pl.loop(0, 4)
    def _(back):
        l = 3 - back
        d, reach = scal[l], scal[16 + l]
        first = 16 - reach + OFF

        @pl.loop(0, 16 + reach)
        def _(q):
            for u in range(2):
                i = first + 2 * q + u
                x = bk[i]
                act[i, :, 0:128] = pltpu.roll(x, 96 - d, 0).astype(BF)
                act[i, :, 128:256] = x.astype(BF)
                act[i, :, 256:384] = pltpu.roll(x, d, 0).astype(BF)

        @pl.loop(0, (32 + 2 * (reach + d) + R - 1) // R)
        def _(c):
            i = first - d + R * c
            total = nn(act[pl.ds(i + d, R)].reshape(R * 96, 384), wb[l, 0:384])
            total = total + nn(act[pl.ds(i, R)].reshape(R * 96, 384), wb[l, 384:768])
            total = total + nn(act[pl.ds(i - d, R)].reshape(R * 96, 384), wb[l, 768:1152])
            bk[pl.ds(i, R)] += slope[l, pl.ds(i, R)].astype(F32) * total.reshape(R, 96, 128)

    if second:
        ga[:, 0:16, :] = jnp.zeros((32, 16, 128), F32)
        ga[:, 80:96, :] = jnp.zeros((32, 16, 128), F32)
        for f in range(8):
            base = 8 * scal[8 + f]
            inside = (base >= 16) & (base < 48)
            grow = jnp.where(inside, base - 16, 0)
            keep = jnp.where(inside, 1.0, 0.0)
            for r in range(8):
                x = bk[base + r + OFF].astype(BF)
                y = (keep * (g[grow + r] + ga[grow + r])).astype(BF)
                x = jnp.concatenate([x, y], axis=1)
                edge = jnp.zeros((16, 256), BF)
                x = jnp.concatenate([edge, x, edge], axis=0)
                outs[f][r] = (-STEP * nt(enc_eye[...], x)).astype(BF)
    else:
        for half in range(2):
            for c in range(2):
                lo = 32 * half + 16 * c
                for sec in range(3):
                    x = bk[lo + OFF : lo + OFF + 16, 32 * sec : 32 * sec + 32, :].reshape(512, 128).astype(BF)
                    if half + c == 1:
                        y = g[lo - 16 : lo, 32 * sec : 32 * sec + 32, :].reshape(512, 128).astype(BF)
                        val = nt(enc_eye[...], jnp.concatenate([x, y], axis=1))
                    else:
                        val = nt(enc_eye[:, 0:128], x)
                    outs[half][:, 1024 * sec + 512 * c : 1024 * sec + 512 * c + 512] = val.astype(BF)
            rows = []
            for col in (32, 63):
                for i in range(32):
                    x = bk[32 * half + i + OFF, col : col + 1, :]
                    here = 32 * half + i - 16
                    if 0 <= here < 32:
                        y = g[here, col : col + 1, :]
                    else:
                        y = jnp.zeros((1, 128), F32)
                    rows.append(jnp.concatenate([x, y], axis=1))
            rows.append(jnp.zeros((64, 256), F32))
            x = jnp.concatenate(rows, axis=0).astype(BF)
            outs[half][:, 3072:3200] = nt(enc_eye[...], x).astype(BF)


def c_own(half, c):
    return 0 if (half, c) == (0, 1) else 1


def iteration(second, scal, count, *arrays):
    smem = pl.BlockSpec(memory_space=pltpu.SMEM)
    vmem = pl.BlockSpec(memory_space=pltpu.VMEM)
    if second:
        shapes = [jax.ShapeDtypeStruct((8, V, 128), BF)] * 8 + [jax.ShapeDtypeStruct((V, 4096), BF)]
    else:
        shapes = [jax.ShapeDtypeStruct((V, 3200), BF)] * 2
    return pl.pallas_call(
        functools.partial(iterate, second),
        out_shape=shapes,
        in_specs=[smem, smem] + [vmem] * len(arrays),
        out_specs=[vmem] * len(shapes),
        scratch_shapes=[
            pltpu.VMEM((64, 128, 128), F32),
            pltpu.VMEM((ROWS, 128, 128), F32),
            pltpu.VMEM((ROWS, 96, 384), BF),
            pltpu.VMEM((4, ROWS, 96, 128), BF),
            pltpu.VMEM((ROWS, 96, 128), F32),
            pltpu.VMEM((V, 3072), BF),
            pltpu.VMEM((3072, 256), BF),
            pltpu.VMEM((32, 96, 128), F32),
            pltpu.VMEM((32, 96, 128), F32),
        ],
        compiler_params=pltpu.CompilerParams(vmem_limit_bytes=VMEM),
        cost_estimate=pl.CostEstimate(flops=10**10, bytes_accessed=6 * 10**6, transcendentals=3 * 10**6),
        name="second_iteration" if second else "first_iteration",
    )(scal, count, *arrays)


def on_device(
    background,
    encoder_weight,
    convolution_weight,
    decoder_weight,
    dilations,
    obs_values,
    obs_prec,
    obs_frac,
    obs_dest,
    obs_cell,
    obs_count,
):
    smem = pl.BlockSpec(memory_space=pltpu.SMEM)
    vmem = pl.BlockSpec(memory_space=pltpu.VMEM)
    lon, lat = lax.axis_index("lon"), lax.axis_index("lat")
    sub = lon % 4
    flip = lat % 2 == 1

    def block_of(s):
        return jnp.where(flip, 3 - s, s)

    k = block_of(sub)
    top = 256 * lat + 64 * k
    came = [(sub - m) % 4 for m in range(4)]
    tables = [c + 2 for c in came] + [jnp.where(c >= 2, c - 2, c + 6) for c in came]
    d = dilations
    scal = jnp.stack(
        [d[0], d[1], d[2], d[3], 32 - top, 2048 + 32 - top, 64 * k, jnp.int32(0)]
        + tables
        + [d[1] + d[2] + d[3], d[2] + d[3], d[3], jnp.int32(0)]
    ).astype(jnp.int32)

    rows = obs_dest.shape[0]
    owner = obs_dest[:, 0]
    group = (owner // 32) * 8 + owner % 8
    member = (group[:, None] == jnp.arange(32, dtype=jnp.int32)[None, :]).astype(BF)
    order = jnp.arange(rows, dtype=jnp.int32)
    earlier = (order[None, :] < order[:, None]).astype(BF)
    rank = jnp.sum(nn(earlier, member) * member.astype(F32), axis=1).astype(jnp.int32)
    slots = group * 32 + rank
    alive = (jnp.arange(rows, dtype=jnp.int32) < obs_count[0]).astype(F32)
    prec = alive * obs_prec
    wide = jnp.stack([prec, obs_frac[0], obs_frac[1]])
    high = wide.astype(BF)
    low = (wide - high.astype(F32)).astype(BF)
    li = 8 * ((owner // 8) % 4) + obs_cell // 255
    lj = obs_cell % 255
    payload = jnp.concatenate(
        [
            obs_values.astype(BF),
            jnp.zeros((3, rows), BF),
            jnp.stack([high[0], low[0], high[1], low[1], high[2], low[2], li.astype(BF), lj.astype(BF)]),
        ]
    )
    pick = (slots[:, None] == jnp.arange(1024, dtype=jnp.int32)[None, :]).astype(BF)
    packed = jnp.einsum("vr,rs->vs", payload, pick, preferred_element_type=F32).astype(BF)
    arrived = lax.all_to_all(packed, AXES, split_axis=1, concat_axis=1, tiled=True, axis_index_groups=GROUPS_32)
    arrived = lax.all_gather(arrived, AXES, axis_index_groups=GROUPS_4)
    comp, posx, count = pl.pallas_call(
        compact_kernel,
        out_shape=[
            jax.ShapeDtypeStruct((80, 4096), BF),
            jax.ShapeDtypeStruct((32, 128), F32),
            jax.ShapeDtypeStruct((1,), jnp.int32),
        ],
        in_specs=[smem, vmem],
        out_specs=[vmem, vmem, smem],
        scratch_shapes=[pltpu.VMEM((32, 128), F32)],
        name="compact",
    )(scal, arrived)

    cells = jnp.pad(background.astype(BF).transpose(1, 0, 2), ((0, 0), (0, V - 69), (0, 0)))
    before = lax.ppermute(cells[:, :, 224:256], AXES, BAND_UP)
    after = lax.ppermute(cells[:, :, 0:32], AXES, BAND_DOWN)
    band = jnp.concatenate([before, cells, after], axis=2)
    parts = jnp.stack([band[:, :, 64 * b : 64 * b + 128] for b in range(4)])
    sends = [lax.dynamic_index_in_dim(parts, block_of((sub + m) % 4), 0, keepdims=False) for m in range(4)]
    chunks = [sends[0]] + [lax.ppermute(sends[m % 4], AXES, family(m)) for m in range(1, 8)]

    eye = jnp.eye(V, 128, dtype=BF)
    enc_v = jnp.pad(encoder_weight.T, ((0, 128 - 69), (0, 0)))
    dec_v = jnp.pad(decoder_weight, ((0, 128 - 69), (0, 0)))
    weights = (
        enc_v,
        jnp.concatenate([enc_v[0:V], eye], axis=1),
        jnp.concatenate([dec_v[0:V], eye], axis=1),
        dec_v,
        eye,
        convolution_weight.transpose(0, 1, 3, 2).reshape(4, 1152, 128),
        convolution_weight.reshape(4, 1152, 128),
    )

    left, right = iteration(False, scal, count, *chunks, *weights, comp)
    left_in = lax.ppermute(right, AXES, LON_UP)
    right_in = lax.ppermute(left, AXES, LON_DOWN)
    left = (left.astype(F32) + left_in.astype(F32)).astype(BF)
    right = (right.astype(F32) + right_in.astype(F32)).astype(BF)
    extra = [left[:, 3072:3200], right[:, 3072:3200]]
    from_next = lax.ppermute(jnp.concatenate([left[:, 0:1024], right[:, 0:1024]] + extra, axis=1), AXES, LAT_DOWN)
    from_prev = lax.ppermute(jnp.concatenate([left[:, 2048:3072], right[:, 2048:3072]] + extra, axis=1), AXES, LAT_UP)
    *moves, found = iteration(True, scal, count, *chunks, *weights, comp, left, right, from_prev, from_next)

    spread = pl.pallas_call(
        expand_kernel,
        out_shape=jax.ShapeDtypeStruct((4, V, 1024), BF),
        in_specs=[smem, vmem, vmem],
        out_specs=vmem,
        scratch_shapes=[pltpu.VMEM((4, V, 1024), F32)],
        name="expand",
    )(count, posx, found)
    spread = lax.all_to_all(spread, AXES, split_axis=0, concat_axis=0, tiled=True, axis_index_groups=GROUPS_4)
    spread = jnp.sum(spread.astype(F32), axis=0).astype(BF)
    spread = lax.all_to_all(spread, AXES, split_axis=1, concat_axis=1, tiled=True, axis_index_groups=GROUPS_32)
    equivalent = jnp.einsum("vs,rs->vr", spread[0:69], pick, preferred_element_type=F32)
    innovation = alive[None, :] * (equivalent - obs_values)

    back = [moves[0]] + [lax.ppermute(moves[m], AXES, [(b, a) for a, b in family(m)]) for m in range(1, 8)]
    total = jnp.zeros((8, V, 320), F32)
    summed = jnp.stack([back[m].astype(F32) + back[m + 4].astype(F32) for m in range(4)])
    for b in range(4):
        m = (jnp.where(flip, 3 - b, b) - sub) % 4
        block = lax.dynamic_index_in_dim(summed, m, 0, keepdims=False)
        total = total + jnp.pad(block, ((0, 0), (0, 0), (64 * b, 192 - 64 * b)))
    edge_up = lax.ppermute(total[:, :, 288:320].astype(BF), AXES, BAND_UP)
    edge_down = lax.ppermute(total[:, :, 0:32].astype(BF), AXES, BAND_DOWN)
    total = total[:, :, 32:288]
    total = total + jnp.pad(edge_up.astype(F32), ((0, 0), (0, 0), (0, 224)))
    total = total + jnp.pad(edge_down.astype(F32), ((0, 0), (0, 0), (224, 0)))
    analysis = background + total[:, 0:69, :].transpose(1, 0, 2)
    return (analysis, innovation)


def solution(mesh):
    placed = (
        P(None, "lon", "lat"),
        P(),
        P(),
        P(),
        P(),
        P(None, ("lon", "lat")),
        P(("lon", "lat")),
        P(None, ("lon", "lat")),
        P(("lon", "lat"), None),
        P(("lon", "lat")),
        P(("lon", "lat")),
    )
    return jax.shard_map(
        on_device,
        mesh=mesh,
        in_specs=placed,
        out_specs=(P(None, "lon", "lat"), P(None, ("lon", "lat"))),
        check_vma=False,
    )
```

```python
import functools

import jax
import jax.numpy as jnp
from jax import lax
from jax.experimental import pallas as pl
from jax.experimental.pallas import tpu as pltpu
from jax.sharding import PartitionSpec as P

AXES = ("lon", "lat")
BF = jnp.bfloat16
F32 = jnp.float32
V = 72
OFF = 8
ROWS = 96
R = 16
STEP = 0.25
VMEM = 60 * 1024 * 1024


def snake(s, lat):
    return s if lat % 2 == 0 else 3 - s


def device(lon, lat):
    return 8 * lon + lat


def worker(y, p):
    lat, k = p // 4, p % 4
    return device(4 * y + snake(k, lat), lat)


LON_UP = [(worker(y, p), worker((y + 1) % 4, p)) for y in range(4) for p in range(32)]
LON_DOWN = [(b, a) for a, b in LON_UP]
LAT_UP = [(worker(y, p), worker(y, p + 1)) for y in range(4) for p in range(31)]
LAT_DOWN = [(b, a) for a, b in LAT_UP]
BAND_UP = [(device(n, l), device(n, l + 1)) for n in range(16) for l in range(7)]
BAND_DOWN = [(b, a) for a, b in BAND_UP]
GROUPS_32 = [[device(4 * y + s, l) for y in range(4) for l in range(8)] for s in range(4)]
GROUPS_4 = [[device(4 * y + s, l) for s in range(4)] for y in range(4) for l in range(8)]


def family(m):
    pairs = []
    for y in range(4):
        for s in range(4):
            to = y if m < 4 else (y + (1 if s >= 2 else -1)) % 4
            for l in range(8):
                pairs.append((device(4 * y + s, l), device(4 * to + (s + m) % 4, l)))
    return pairs


def nt(a, b):
    return lax.dot_general(a, b, (((1,), (1,)), ((), ())), preferred_element_type=F32)


def tn(a, b):
    return lax.dot_general(a, b, (((0,), (0,)), ((), ())), preferred_element_type=F32)


def nn(a, b):
    return jnp.dot(a, b, preferred_element_type=F32)


def compact_kernel(scal, pay0, pay1, pay2, pay3, comp, posx, count, total):
    pays = (pay0, pay1, pay2, pay3)
    k64 = scal[6].astype(F32)
    mine, own = [], []
    for part in range(4):
        ctrl = pays[part][...].astype(F32)[72:80]
        local = ctrl[7:8] - k64
        live = ctrl[0:1] > 0.0
        mine.append(jnp.where(live & (local >= -1.0) & (local <= 63.0), 1.0, 0.0))
        own.append(jnp.where(live & (local >= 0.0) & (local <= 63.0), 1.0, 0.0))
    mine = jnp.concatenate([m[:, 128 * c : 128 * c + 128] for m in mine for c in range(8)], axis=0)
    own = jnp.concatenate([m[:, 128 * c : 128 * c + 128] for m in own for c in range(8)], axis=0)
    row = lax.broadcasted_iota(jnp.int32, (128, 128), 0)
    col = lax.broadcasted_iota(jnp.int32, (128, 128), 1)
    before = nn(mine.astype(BF), jnp.where(row < col, 1.0, 0.0).astype(BF))
    sums = nn(mine.astype(BF), jnp.ones((128, 128), BF))
    row4 = lax.broadcasted_iota(jnp.int32, (32, 32), 0)
    col4 = lax.broadcasted_iota(jnp.int32, (32, 32), 1)
    offset = nn(jnp.where(col4 < row4, 1.0, 0.0).astype(BF), sums.astype(BF))
    place = before + offset
    owned = jnp.where(own > 0.0, place, -1.0)
    for m in range(4):
        posx[pl.ds(pl.multiple_of(8 * (scal[8 + m] - 2), 8), 8), :] = owned[8 * m : 8 * m + 8]
    total[...] = jnp.where(mine > 0.0, place, -1.0)
    number = jnp.sum(mine).astype(jnp.int32)
    count[0] = number
    comp[...] = jnp.zeros_like(comp)
    index = lax.broadcasted_iota(jnp.int32, (256, 128), 0).astype(F32)

    @pl.loop(0, (number + 255) // 256)
    def _(tile):
        ids = index + (tile * 256).astype(F32)
        out = jnp.zeros((80, 256), F32)
        for c in range(0, 32, 2):
            picks = jnp.concatenate(
                [jnp.where(ids == total[c + h : c + h + 1, :], 1.0, 0.0).astype(BF) for h in (0, 1)], axis=1
            )
            out = out + nt(pays[c // 8][:, 128 * (c % 8) : 128 * (c % 8) + 256], picks)
        comp[:, pl.ds(pl.multiple_of(tile * 256, 256), 256)] = out.astype(BF)


def expand_kernel(count, posx, found, out, total):
    index = lax.broadcasted_iota(jnp.int32, (256, 128), 0).astype(F32)
    total[...] = jnp.zeros_like(total)

    @pl.loop(0, (count[0] + 255) // 256)
    def _(tile):
        ids = index + (tile * 256).astype(F32)
        rows = found[:, pl.ds(pl.multiple_of(tile * 256, 256), 256)]
        for c in range(32):
            picks = jnp.where(ids == posx[c : c + 1, :], 1.0, 0.0).astype(BF)
            to = 128 * (8 * (c % 8 // 2) + 2 * (c // 8) + c % 2)
            total[:, to : to + 128] += nn(rows, picks)

    out[...] = total[...].astype(BF)


def convolve(act, weight, d, first, count, store):
    for dd in range(1, 5):
        blocks = 8 // dd
        step = 2 * blocks * dd

        @pl.when(d == dd)
        def _():
            @pl.loop(0, (count + step - 1) // step)
            def _(c):
                i = first + step * c
                x = act[pl.ds(i - dd, step + 2 * dd)].reshape(blocks + 1, 2, dd, 96, 384)
                m = blocks * dd * 96
                x = [x[p // 2 : p // 2 + blocks, p % 2].reshape(m, 384) for p in range(4)]
                y = nn(jnp.concatenate(x, axis=1), weight[...])
                y = jnp.stack([y[:, 128 * p : 128 * p + 128].reshape(blocks, dd, 96, 128) for p in (0, 1)], axis=1)
                store(pl.ds(i, step), y.reshape(step, 96, 128))


def iterate(second, *refs):
    scal, count = refs[0:2]
    chunks = refs[2:10]
    enc_t, enc_eye, dec_eye, dec_n, eye, wf, wb, comp = refs[10:18]
    refs = refs[18:]
    if second:
        tots, from_prev, from_next = refs[0:2], refs[2], refs[3]
        outs, found = refs[4:12], refs[12]
        refs = refs[13:]
    else:
        outs = refs[0:2]
        refs = refs[2:]
    st, h, act, slope, bk, fct, wobs, g, ga, shift = refs

    act[...] = jnp.zeros_like(act)

    for f in range(8):
        base = 8 * scal[8 + f]
        for r in range(8):
            st[base + r] = tn(chunks[f][r], eye[...])
    if second:
        for half in range(2):
            tot = tots[half]
            for c in range(2):
                rows = pl.ds(32 * half + 16 * c, 16)
                lanes = 1024 * half + 512 * c
                for sec in range(3):
                    add = tot[:, 1024 * sec + 512 * c : 1024 * sec + 512 * c + 512].astype(F32)
                    if sec == 0:
                        add = add + from_prev[:, lanes : lanes + 512].astype(F32)
                    if sec == 2:
                        add = add + from_next[:, lanes : lanes + 512].astype(F32)
                    add = tn(add.astype(BF), eye[...]).reshape(16, 32, 128)
                    st[rows, 16 + 32 * sec : 48 + 32 * sec, :] -= STEP * add
                    if half + c == 1:
                        ga[pl.ds(16 * c_own(half, c), 16), 32 * sec : 32 * sec + 32, :] = 0.75 * add
            low = tn(from_prev[:, 2048 + 128 * half : 2176 + 128 * half], eye[...])
            high = tn(from_next[:, 2048 + 128 * half : 2176 + 128 * half], eye[...])
            for i in range(32):
                st[32 * half + i, 15:16, :] -= STEP * low[32 + i : 33 + i]
                st[32 * half + i, 112:113, :] -= STEP * high[i : i + 1]

    @pl.loop(0, 8)
    def _(c):
        x = st[pl.ds(8 * c, 8)].reshape(1024, 128).astype(BF)
        h[pl.ds(8 * c + OFF, 8)] = nn(x, enc_t[...]).reshape(8, 128, 128)

    e = lax.broadcasted_iota(jnp.int32, (112, 128), 0) + 8
    mask = jnp.where((e >= scal[4]) & (e < scal[5]), 1.0, 0.0)

    @pl.loop(0, 4)
    def _(l):
        d, reach = scal[l], scal[16 + l]
        first = 16 - reach - d + OFF

        @pl.loop(0, 16 + reach + d)
        def _(q):
            for u in range(2):
                i = first + 2 * q + u
                t = jnp.tanh(h[i, 8:120, :])
                slope[l, i] = ((1.0 - t * t) * mask)[8:104].astype(BF)
                t = t * mask
                shift[u] = t
                act[i, :, 0:128] = shift[u, pl.ds(8 - d, 96), :].astype(BF)
                act[i, :, 128:256] = t[8:104].astype(BF)
                act[i, :, 256:384] = shift[u, pl.ds(8 + d, 96), :].astype(BF)

        for u in range(R):
            slope[l, 48 + reach + d + OFF + u] = jnp.zeros((96, 128), BF)

        def store(rows, y):
            h[rows, 16:112, :] += y

        convolve(act, wf.at[l], d, 16 - reach + OFF, 32 + 2 * reach, store)

    for c in range(4):
        a = h[16 + OFF + 8 * c : 24 + OFF + 8 * c, 16:112, :].reshape(768, 128).astype(BF)
        b = st[16 + 8 * c : 24 + 8 * c, 16:112, :].reshape(768, 128).astype(BF)
        fct[:, 768 * c : 768 * c + 768] = nt(dec_eye[...], jnp.concatenate([a, b], axis=1)).astype(BF)

    g[...] = jnp.zeros_like(g)
    k64 = scal[6].astype(F32)
    lon_of = lax.broadcasted_iota(jnp.int32, (32, 256), 0).astype(F32)
    lat_of = lax.broadcasted_iota(jnp.int32, (96, 256), 0).astype(F32) - 16.0

    @pl.loop(0, (count[0] + 255) // 256)
    def _(tile):
        lanes = pl.ds(pl.multiple_of(tile * 256, 256), 256)
        pay = comp[:, lanes].astype(F32)
        prec = pay[72:73] + pay[73:74]
        fu = pay[74:75] + pay[75:76]
        fv = pay[76:77] + pay[77:78]
        li, lj = pay[78:79], pay[79:80] - k64
        wa = jnp.where(lon_of == li, 1.0 - fu, 0.0) + jnp.where(lon_of == li + 1.0, fu, 0.0)
        wl = (jnp.where(lat_of == lj, 1.0 - fv, 0.0) + jnp.where(lat_of == lj + 1.0, fv, 0.0)).astype(BF)
        wa = wa.astype(BF)
        for i in range(32):
            wobs[96 * i : 96 * i + 96, :] = wa[i : i + 1] * wl
        eq = nn(fct[...], wobs[...])
        if second:
            found[:, lanes] = eq.astype(BF)
        wt = (prec * (eq - pay[0:72])).astype(BF)
        wt = jnp.concatenate([wt, jnp.zeros((56, 256), BF)], axis=0)
        for c in range(4):
            g[pl.ds(8 * c, 8)] += nt(wobs[768 * c : 768 * c + 768, :], wt).reshape(8, 96, 128)

    g[:, 0:16, :] = jnp.zeros((32, 16, 128), F32)
    g[:, 80:96, :] = jnp.zeros((32, 16, 128), F32)

    bk[...] = jnp.zeros_like(bk)
    act[0:24] = jnp.zeros((24, 96, 384), BF)
    act[56:96] = jnp.zeros((40, 96, 384), BF)
    for c in range(4):
        x = g[8 * c : 8 * c + 8].reshape(768, 128).astype(BF)
        bk[16 + OFF + 8 * c : 24 + OFF + 8 * c, 8:104, :] = nn(x, dec_n[...]).reshape(8, 96, 128)

    @pl.loop(0, 4)
    def _(back):
        l = 3 - back
        d, reach = scal[l], scal[16 + l]
        first = 16 - reach + OFF

        @pl.loop(0, 16 + reach)
        def _(q):
            for u in range(2):
                i = first + 2 * q + u
                act[i, :, 0:128] = bk[i, pl.ds(8 - d, 96), :].astype(BF)
                act[i, :, 128:256] = bk[i, 8:104, :].astype(BF)
                act[i, :, 256:384] = bk[i, pl.ds(8 + d, 96), :].astype(BF)

        def store(rows, y):
            bk[rows, 8:104, :] += slope[l, rows].astype(F32) * y

        convolve(act, wb.at[l], d, first - d, 32 + 2 * (reach + d), store)

    if second:
        ga[:, 0:16, :] = jnp.zeros((32, 16, 128), F32)
        ga[:, 80:96, :] = jnp.zeros((32, 16, 128), F32)
        for f in range(8):
            base = 8 * scal[8 + f]
            inside = (base >= 16) & (base < 48)
            grow = jnp.where(inside, base - 16, 0)
            keep = jnp.where(inside, 1.0, 0.0)
            for r in range(8):
                x = bk[base + r + OFF, 8:104, :].astype(BF)
                y = (keep * (g[grow + r] + ga[grow + r])).astype(BF)
                x = jnp.concatenate([x, y], axis=1)
                edge = jnp.zeros((16, 256), BF)
                x = jnp.concatenate([edge, x, edge], axis=0)
                outs[f][r] = (-STEP * nt(enc_eye[...], x)).astype(BF)
    else:
        for half in range(2):
            for c in range(2):
                lo = 32 * half + 16 * c
                for sec in range(3):
                    x = bk[lo + OFF : lo + OFF + 16, 32 * sec + 8 : 32 * sec + 40, :].reshape(512, 128).astype(BF)
                    if half + c == 1:
                        y = g[lo - 16 : lo, 32 * sec : 32 * sec + 32, :].reshape(512, 128).astype(BF)
                        val = nt(enc_eye[...], jnp.concatenate([x, y], axis=1))
                    else:
                        val = nt(enc_eye[:, 0:128], x)
                    outs[half][:, 1024 * sec + 512 * c : 1024 * sec + 512 * c + 512] = val.astype(BF)
            rows = []
            for col in (32, 63):
                for i in range(32):
                    x = bk[32 * half + i + OFF, col + 8 : col + 9, :]
                    here = 32 * half + i - 16
                    if 0 <= here < 32:
                        y = g[here, col : col + 1, :]
                    else:
                        y = jnp.zeros((1, 128), F32)
                    rows.append(jnp.concatenate([x, y], axis=1))
            rows.append(jnp.zeros((64, 256), F32))
            x = jnp.concatenate(rows, axis=0).astype(BF)
            outs[half][:, 3072:3200] = nt(enc_eye[...], x).astype(BF)


def c_own(half, c):
    return 0 if (half, c) == (0, 1) else 1


def iteration(second, scal, count, *arrays):
    smem = pl.BlockSpec(memory_space=pltpu.SMEM)
    vmem = pl.BlockSpec(memory_space=pltpu.VMEM)
    if second:
        shapes = [jax.ShapeDtypeStruct((8, V, 128), BF)] * 8 + [jax.ShapeDtypeStruct((V, 4096), BF)]
    else:
        shapes = [jax.ShapeDtypeStruct((V, 3200), BF)] * 2
    return pl.pallas_call(
        functools.partial(iterate, second),
        out_shape=shapes,
        in_specs=[smem, smem] + [vmem] * len(arrays),
        out_specs=[vmem] * len(shapes),
        scratch_shapes=[
            pltpu.VMEM((64, 128, 128), F32),
            pltpu.VMEM((ROWS, 128, 128), F32),
            pltpu.VMEM((ROWS, 96, 384), BF),
            pltpu.VMEM((4, ROWS, 96, 128), BF),
            pltpu.VMEM((ROWS, 112, 128), F32),
            pltpu.VMEM((V, 3072), BF),
            pltpu.VMEM((3072, 256), BF),
            pltpu.VMEM((32, 96, 128), F32),
            pltpu.VMEM((32, 96, 128), F32),
            pltpu.VMEM((2, 112, 128), F32),
        ],
        compiler_params=pltpu.CompilerParams(vmem_limit_bytes=VMEM),
        cost_estimate=pl.CostEstimate(flops=10**10, bytes_accessed=6 * 10**6, transcendentals=3 * 10**6),
        name="second_iteration" if second else "first_iteration",
    )(scal, count, *arrays)


def paired(taps):
    none = jnp.zeros((taps.shape[0], 384, 128), BF)
    low, mid, top = taps[:, 0], taps[:, 1], taps[:, 2]
    first = jnp.concatenate([low, mid, top, none], axis=1)
    later = jnp.concatenate([none, low, mid, top], axis=1)
    return jnp.concatenate([first, later], axis=2)


def make_weights(encoder_weight, convolution_weight, decoder_weight):
    eye = jnp.eye(V, 128, dtype=BF)
    enc_v = jnp.pad(encoder_weight.T, ((0, 128 - 69), (0, 0)))
    dec_v = jnp.pad(decoder_weight, ((0, 128 - 69), (0, 0)))
    ahead = convolution_weight.transpose(0, 1, 3, 2).reshape(4, 3, 384, 128)
    back = convolution_weight[:, ::-1].reshape(4, 3, 384, 128)
    return (
        enc_v,
        jnp.concatenate([enc_v[0:V], eye], axis=1),
        jnp.concatenate([dec_v[0:V], eye], axis=1),
        dec_v,
        eye,
        paired(ahead),
        paired(back),
    )


def on_device(
    background,
    encoder_weight,
    convolution_weight,
    decoder_weight,
    dilations,
    obs_values,
    obs_prec,
    obs_frac,
    obs_dest,
    obs_cell,
    obs_count,
):
    smem = pl.BlockSpec(memory_space=pltpu.SMEM)
    vmem = pl.BlockSpec(memory_space=pltpu.VMEM)
    lon, lat = lax.axis_index("lon"), lax.axis_index("lat")
    sub = lon % 4
    flip = lat % 2 == 1

    def block_of(s):
        return jnp.where(flip, 3 - s, s)

    k = block_of(sub)
    top = 256 * lat + 64 * k
    came = [(sub - m) % 4 for m in range(4)]
    tables = [c + 2 for c in came] + [jnp.where(c >= 2, c - 2, c + 6) for c in came]
    d = dilations
    scal = jnp.stack(
        [d[0], d[1], d[2], d[3], 32 - top, 2048 + 32 - top, 64 * k, jnp.int32(0)]
        + tables
        + [d[1] + d[2] + d[3], d[2] + d[3], d[3], jnp.int32(0)]
    ).astype(jnp.int32)

    rows = obs_dest.shape[0]
    owner = obs_dest[:, 0]
    group = (owner // 32) * 8 + owner % 8
    member = (group[:, None] == jnp.arange(32, dtype=jnp.int32)[None, :]).astype(BF)
    order = jnp.arange(rows, dtype=jnp.int32)
    earlier = (order[None, :] < order[:, None]).astype(BF)
    rank = jnp.sum(nn(earlier, member) * member.astype(F32), axis=1).astype(jnp.int32)
    slots = group * 32 + rank
    alive = (jnp.arange(rows, dtype=jnp.int32) < obs_count[0]).astype(F32)
    prec = alive * obs_prec
    wide = jnp.stack([prec, obs_frac[0], obs_frac[1]])
    high = wide.astype(BF)
    low = (wide - high.astype(F32)).astype(BF)
    li = 8 * ((owner // 8) % 4) + obs_cell // 255
    lj = obs_cell % 255
    payload = jnp.concatenate(
        [
            obs_values.astype(BF),
            jnp.zeros((3, rows), BF),
            jnp.stack([high[0], low[0], high[1], low[1], high[2], low[2], li.astype(BF), lj.astype(BF)]),
        ]
    )
    pick = (slots[:, None] == jnp.arange(1024, dtype=jnp.int32)[None, :]).astype(BF)
    packed = jnp.einsum("vr,rs->vs", payload, pick, preferred_element_type=F32).astype(BF)
    arrived = lax.all_to_all(packed, AXES, split_axis=1, concat_axis=1, tiled=True, axis_index_groups=GROUPS_32)
    others = [
        lax.ppermute(arrived, AXES, [(g[s], g[(s + m) % 4]) for g in GROUPS_4 for s in range(4)]) for m in range(1, 4)
    ]
    comp, posx, count = pl.pallas_call(
        compact_kernel,
        out_shape=[
            jax.ShapeDtypeStruct((80, 4096), BF),
            jax.ShapeDtypeStruct((32, 128), F32),
            jax.ShapeDtypeStruct((1,), jnp.int32),
        ],
        in_specs=[smem] + [vmem] * 4,
        out_specs=[vmem, vmem, smem],
        scratch_shapes=[pltpu.VMEM((32, 128), F32)],
        name="compact",
    )(scal, arrived, *others)

    cells = jnp.pad(background.astype(BF).transpose(1, 0, 2), ((0, 0), (0, V - 69), (0, 0)))
    before = lax.ppermute(cells[:, :, 224:256], AXES, BAND_UP)
    after = lax.ppermute(cells[:, :, 0:32], AXES, BAND_DOWN)
    band = jnp.concatenate([before, cells, after], axis=2)
    parts = jnp.stack([band[:, :, 64 * b : 64 * b + 128] for b in range(4)])
    sends = [lax.dynamic_index_in_dim(parts, block_of((sub + m) % 4), 0, keepdims=False) for m in range(4)]
    chunks = [sends[0]] + [lax.ppermute(sends[m % 4], AXES, family(m)) for m in range(1, 8)]

    weights = make_weights(encoder_weight, convolution_weight, decoder_weight)

    left, right = iteration(False, scal, count, *chunks, *weights, comp)
    left_in = lax.ppermute(right, AXES, LON_UP)
    right_in = lax.ppermute(left, AXES, LON_DOWN)
    left = (left.astype(F32) + left_in.astype(F32)).astype(BF)
    right = (right.astype(F32) + right_in.astype(F32)).astype(BF)
    extra = [left[:, 3072:3200], right[:, 3072:3200]]
    from_next = lax.ppermute(jnp.concatenate([left[:, 0:1024], right[:, 0:1024]] + extra, axis=1), AXES, LAT_DOWN)
    from_prev = lax.ppermute(jnp.concatenate([left[:, 2048:3072], right[:, 2048:3072]] + extra, axis=1), AXES, LAT_UP)
    *moves, found = iteration(True, scal, count, *chunks, *weights, comp, left, right, from_prev, from_next)

    spread = pl.pallas_call(
        expand_kernel,
        out_shape=jax.ShapeDtypeStruct((V, 4096), BF),
        in_specs=[smem, vmem, vmem],
        out_specs=vmem,
        scratch_shapes=[pltpu.VMEM((V, 4096), F32)],
        name="expand",
    )(count, posx, found)
    *moves, spread = lax.optimization_barrier((*moves, spread))
    spread = lax.all_to_all(spread, AXES, split_axis=1, concat_axis=1, tiled=True)
    spread = [spread[:, 256 * c : 256 * c + 256] for c in range(16)]
    spread = jnp.concatenate(
        [spread[4 * y] + spread[4 * y + 1] + spread[4 * y + 2] + spread[4 * y + 3] for y in range(4)], axis=1
    )
    equivalent = jnp.einsum("vs,rs->vr", spread[0:69], pick, preferred_element_type=F32)
    innovation = alive[None, :] * (equivalent - obs_values)

    back = [moves[0]] + [lax.ppermute(moves[m], AXES, [(b, a) for a, b in family(m)]) for m in range(1, 8)]
    total = jnp.zeros((8, V, 320), F32)
    summed = jnp.stack([back[m].astype(F32) + back[m + 4].astype(F32) for m in range(4)])
    for b in range(4):
        m = (jnp.where(flip, 3 - b, b) - sub) % 4
        block = lax.dynamic_index_in_dim(summed, m, 0, keepdims=False)
        total = total + jnp.pad(block, ((0, 0), (0, 0), (64 * b, 192 - 64 * b)))
    edge_up = lax.ppermute(total[:, :, 288:320].astype(BF), AXES, BAND_UP)
    edge_down = lax.ppermute(total[:, :, 0:32].astype(BF), AXES, BAND_DOWN)
    total = total[:, :, 32:288]
    total = total + jnp.pad(edge_up.astype(F32), ((0, 0), (0, 0), (0, 224)))
    total = total + jnp.pad(edge_down.astype(F32), ((0, 0), (0, 0), (224, 0)))
    analysis = background + total[:, 0:69, :].transpose(1, 0, 2)
    return (analysis, innovation)


def solution(mesh):
    placed = (
        P(None, "lon", "lat"),
        P(),
        P(),
        P(),
        P(),
        P(None, ("lon", "lat")),
        P(("lon", "lat")),
        P(None, ("lon", "lat")),
        P(("lon", "lat"), None),
        P(("lon", "lat")),
        P(("lon", "lat")),
    )
    return jax.shard_map(
        on_device,
        mesh=mesh,
        in_specs=placed,
        out_specs=(P(None, "lon", "lat"), P(None, ("lon", "lat"))),
        check_vma=False,
    )
```

```python
import functools

import jax
import jax.numpy as jnp
from jax import lax
from jax.experimental import pallas as pl
from jax.experimental.pallas import tpu as pltpu
from jax.sharding import PartitionSpec as P

AXES = ("lon", "lat")
BF = jnp.bfloat16
F32 = jnp.float32
V = 72
OFF = 8
ROWS = 96
R = 16
STEP = 0.25
VMEM = 60 * 1024 * 1024


def snake(s, lat):
    return s if lat % 2 == 0 else 3 - s


def device(lon, lat):
    return 8 * lon + lat


def worker(y, p):
    lat, k = p // 4, p % 4
    return device(4 * y + snake(k, lat), lat)


LON_UP = [(worker(y, p), worker((y + 1) % 4, p)) for y in range(4) for p in range(32)]
LON_DOWN = [(b, a) for a, b in LON_UP]
LAT_UP = [(worker(y, p), worker(y, p + 1)) for y in range(4) for p in range(31)]
LAT_DOWN = [(b, a) for a, b in LAT_UP]
BAND_UP = [(device(n, l), device(n, l + 1)) for n in range(16) for l in range(7)]
BAND_DOWN = [(b, a) for a, b in BAND_UP]
GROUPS_32 = [[device(4 * y + s, l) for y in range(4) for l in range(8)] for s in range(4)]
GROUPS_4 = [[device(4 * y + s, l) for s in range(4)] for y in range(4) for l in range(8)]


def family(m):
    pairs = []
    for y in range(4):
        for s in range(4):
            to = y if m < 4 else (y + (1 if s >= 2 else -1)) % 4
            for l in range(8):
                pairs.append((device(4 * y + s, l), device(4 * to + (s + m) % 4, l)))
    return pairs


def turn(m):
    return [(g[s], g[(s + m) % 4]) for g in GROUPS_4 for s in range(4)]


def nt(a, b):
    return lax.dot_general(a, b, (((1,), (1,)), ((), ())), preferred_element_type=F32)


def tn(a, b):
    return lax.dot_general(a, b, (((0,), (0,)), ((), ())), preferred_element_type=F32)


def nn(a, b):
    return jnp.dot(a, b, preferred_element_type=F32)


def pack_kernel(values, prec, frac, dest, cell, packed, slots):
    rows = dest.shape[1]
    owner = dest[...]
    group = lax.shift_right_logical(owner, 5) * 8 + (owner & 7)
    member = lax.broadcasted_iota(jnp.int32, (32, rows), 0) == group
    row = lax.broadcasted_iota(jnp.int32, (rows, rows), 0)
    col = lax.broadcasted_iota(jnp.int32, (rows, rows), 1)
    before = nn(jnp.where(member, 1.0, 0.0).astype(BF), jnp.where(row < col, 1.0, 0.0).astype(BF))
    rank = jnp.sum(jnp.where(member, before, 0.0), axis=0, keepdims=True)
    slot = group * 32 + rank.astype(jnp.int32)
    slots[...] = slot
    lon = jnp.zeros((1, rows), F32)
    code = cell[...]
    for step in range(1, 7):
        lon = lon + jnp.where(code >= 255 * step, 1.0, 0.0)
    lat = code.astype(F32) - 255.0 * lon
    lon = lon + 8.0 * (lax.shift_right_logical(owner, 3) & 3).astype(F32)
    parts = []
    for x in (prec[...], frac[0:1], frac[1:2]):
        high = x.astype(BF).astype(F32)
        parts += [high, x - high]
    ctrl = jnp.concatenate(parts + [lon, lat], axis=0)
    payload = jnp.concatenate([values[...], jnp.zeros((3, rows), F32), ctrl], axis=0).astype(BF)
    for c in range(4):
        index = lax.broadcasted_iota(jnp.int32, (256, rows), 0) + 256 * c
        pick = jnp.where(index == slot, 1.0, 0.0).astype(BF)
        packed[:, 256 * c : 256 * c + 256] = nt(payload, pick).astype(BF)


def split_kernel(scal, cells, before, after, *outs):
    for b in range(4):
        for m in range(4):
            @pl.when(scal[20 + m] == b)
            def _():
                for r in range(8):
                    if b == 0:
                        x = jnp.concatenate([before[r], cells[r, :, 0:96]], axis=1)
                    elif b == 3:
                        x = jnp.concatenate([cells[r, :, 160:256], after[r]], axis=1)
                    else:
                        x = cells[r, :, 64 * b - 32 : 64 * b + 96]
                    outs[m][r] = x


def compact_kernel(scal, pay0, pay1, pay2, pay3, comp, posx, count, total):
    pays = (pay0, pay1, pay2, pay3)
    k64 = scal[6].astype(F32)
    mine, own = [], []
    for part in range(4):
        ctrl = pays[part][...].astype(F32)[72:80]
        local = ctrl[7:8] - k64
        live = ctrl[0:1] > 0.0
        mine.append(jnp.where(live & (local >= -1.0) & (local <= 63.0), 1.0, 0.0))
        own.append(jnp.where(live & (local >= 0.0) & (local <= 63.0), 1.0, 0.0))
    mine = jnp.concatenate([m[:, 128 * c : 128 * c + 128] for m in mine for c in range(8)], axis=0)
    own = jnp.concatenate([m[:, 128 * c : 128 * c + 128] for m in own for c in range(8)], axis=0)
    row = lax.broadcasted_iota(jnp.int32, (128, 128), 0)
    col = lax.broadcasted_iota(jnp.int32, (128, 128), 1)
    before = nn(mine.astype(BF), jnp.where(row < col, 1.0, 0.0).astype(BF))
    sums = nn(mine.astype(BF), jnp.ones((128, 128), BF))
    row4 = lax.broadcasted_iota(jnp.int32, (32, 32), 0)
    col4 = lax.broadcasted_iota(jnp.int32, (32, 32), 1)
    offset = nn(jnp.where(col4 < row4, 1.0, 0.0).astype(BF), sums.astype(BF))
    place = before + offset
    owned = jnp.where(own > 0.0, place, -1.0)
    for m in range(4):
        to = 8 * ((4 - m) % 4)
        posx[to : to + 8, :] = owned[8 * m : 8 * m + 8]
    total[...] = jnp.where(mine > 0.0, place, -1.0)
    number = jnp.sum(mine).astype(jnp.int32)
    count[0] = number
    comp[...] = jnp.zeros_like(comp)
    index = lax.broadcasted_iota(jnp.int32, (256, 128), 0).astype(F32)

    @pl.loop(0, (number + 255) // 256)
    def _(tile):
        ids = index + (tile * 256).astype(F32)
        out = jnp.zeros((80, 256), F32)
        for c in range(0, 32, 2):
            picks = jnp.concatenate(
                [jnp.where(ids == total[c + h : c + h + 1, :], 1.0, 0.0).astype(BF) for h in (0, 1)], axis=1
            )
            out = out + nt(pays[c // 8][:, 128 * (c % 8) : 128 * (c % 8) + 256], picks)
        comp[:, pl.ds(pl.multiple_of(tile * 256, 256), 256)] = out.astype(BF)


def expand_kernel(count, posx, found, *refs):
    outs, total = refs[0:4], refs[4]
    index = lax.broadcasted_iota(jnp.int32, (256, 128), 0).astype(F32)
    total[...] = jnp.zeros_like(total)

    @pl.loop(0, (count[0] + 255) // 256)
    def _(tile):
        ids = index + (tile * 256).astype(F32)
        rows = found[:, pl.ds(pl.multiple_of(tile * 256, 256), 256)]
        for c in range(32):
            picks = jnp.where(ids == posx[c : c + 1, :], 1.0, 0.0).astype(BF)
            total[:, 128 * c : 128 * c + 128] += nn(rows, picks)

    for m in range(4):
        outs[m][...] = total[:, 1024 * m : 1024 * m + 1024].astype(BF)


def convolve(act, weight, d, first, count, store):
    for dd in range(1, 5):
        blocks = 8 // dd
        step = 2 * blocks * dd

        @pl.when(d == dd)
        def _():
            @pl.loop(0, (count + step - 1) // step)
            def _(c):
                i = first + step * c
                x = act[pl.ds(i - dd, step + 2 * dd)].reshape(blocks + 1, 2, dd, 96, 384)
                m = blocks * dd * 96
                x = [x[p // 2 : p // 2 + blocks, p % 2].reshape(m, 384) for p in range(4)]
                y = nn(jnp.concatenate(x, axis=1), weight[...])
                y = jnp.stack([y[:, 128 * p : 128 * p + 128].reshape(blocks, dd, 96, 128) for p in (0, 1)], axis=1)
                store(pl.ds(i, step), y.reshape(step, 96, 128))


def iterate(second, *refs):
    scal, count = refs[0:2]
    chunks = refs[2:10]
    enc_eye, dec_eye, dec_n, wf, wb, comp = refs[10:16]
    refs = refs[16:]
    if second:
        tots, from_prev, from_next = refs[0:2], refs[2], refs[3]
        outs, found = refs[4:12], refs[12]
        refs = refs[13:]
    else:
        outs = refs[0:2]
        refs = refs[2:]
    st, h, act, slope, bk, fct, wobs, g, ga, shift = refs

    act[60:96] = jnp.zeros((36, 96, 384), BF)

    for f in range(8):
        base = 8 * scal[8 + f]
        for r in range(8):
            both = tn(chunks[f][r], enc_eye[...])
            h[base + r + OFF] = both[:, 0:128]
            st[base + r] = both[16:112, 128:256]
    if second:
        for half in range(2):
            tot = tots[half]
            for c in range(2):
                row = 32 * half + 16 * c
                lanes = 1024 * half + 512 * c
                for sec in range(3):
                    add = tot[:, 1024 * sec + 512 * c : 1024 * sec + 512 * c + 512].astype(F32)
                    if sec == 0:
                        add = add + from_prev[:, lanes : lanes + 512].astype(F32)
                    if sec == 2:
                        add = add + from_next[:, lanes : lanes + 512].astype(F32)
                    both = tn(add.astype(BF), enc_eye[...]).reshape(16, 32, 256)
                    h[row + OFF : row + OFF + 16, 16 + 32 * sec : 48 + 32 * sec, :] -= STEP * both[:, :, 0:128]
                    if half + c == 1:
                        st[row : row + 16, 32 * sec : 32 + 32 * sec, :] -= STEP * both[:, :, 128:256]
                        ga[row - 16 : row, 32 * sec : 32 * sec + 32, :] = 0.75 * both[:, :, 128:256]
            low = tn(from_prev[:, 2048 + 128 * half : 2176 + 128 * half], enc_eye[:, 0:128])
            high = tn(from_next[:, 2048 + 128 * half : 2176 + 128 * half], enc_eye[:, 0:128])
            for i in range(32):
                h[32 * half + i + OFF, 15:16, :] -= STEP * low[32 + i : 33 + i]
                h[32 * half + i + OFF, 112:113, :] -= STEP * high[i : i + 1]

    e = lax.broadcasted_iota(jnp.int32, (112, 128), 0) + 8
    mask = jnp.where((e >= scal[4]) & (e < scal[5]), 1.0, 0.0)

    @pl.loop(0, 4)
    def _(l):
        d, reach = scal[l], scal[16 + l]
        first = 16 - reach - d + OFF

        @pl.loop(0, 16 + reach + d)
        def _(q):
            for u in range(2):
                i = first + 2 * q + u
                t = jnp.tanh(h[i, 8:120, :])
                slope[l, i] = ((1.0 - t * t) * mask)[8:104].astype(BF)
                t = t * mask
                shift[u] = t
                act[i, :, 0:128] = shift[u, pl.ds(8 - d, 96), :].astype(BF)
                act[i, :, 128:256] = t[8:104].astype(BF)
                act[i, :, 256:384] = shift[u, pl.ds(8 + d, 96), :].astype(BF)

        for u in range(R):
            slope[l, 48 + reach + d + OFF + u] = jnp.zeros((96, 128), BF)

        def store(rows, y):
            h[rows, 16:112, :] += y

        convolve(act, wf.at[l], d, 16 - reach + OFF, 32 + 2 * reach, store)

    for c in range(4):
        a = h[16 + OFF + 8 * c : 24 + OFF + 8 * c, 16:112, :].reshape(768, 128).astype(BF)
        b = st[16 + 8 * c : 24 + 8 * c].reshape(768, 128).astype(BF)
        fct[:, 768 * c : 768 * c + 768] = nt(dec_eye[...], jnp.concatenate([a, b], axis=1)).astype(BF)

    g[...] = jnp.zeros_like(g)
    k64 = scal[6].astype(F32)
    lon_of = lax.broadcasted_iota(jnp.int32, (32, 256), 0).astype(F32)
    lat_of = lax.broadcasted_iota(jnp.int32, (96, 256), 0).astype(F32) - 16.0

    @pl.loop(0, (count[0] + 255) // 256)
    def _(tile):
        lanes = pl.ds(pl.multiple_of(tile * 256, 256), 256)
        pay = comp[:, lanes].astype(F32)
        prec = pay[72:73] + pay[73:74]
        fu = pay[74:75] + pay[75:76]
        fv = pay[76:77] + pay[77:78]
        li, lj = pay[78:79], pay[79:80] - k64
        wa = jnp.where(lon_of == li, 1.0 - fu, 0.0) + jnp.where(lon_of == li + 1.0, fu, 0.0)
        wl = (jnp.where(lat_of == lj, 1.0 - fv, 0.0) + jnp.where(lat_of == lj + 1.0, fv, 0.0)).astype(BF)
        wa = wa.astype(BF)
        for i in range(32):
            wobs[96 * i : 96 * i + 96, :] = wa[i : i + 1] * wl
        eq = nn(fct[...], wobs[...])
        if second:
            found[:, lanes] = eq.astype(BF)
        wt = (prec * (eq - pay[0:72])).astype(BF)
        wt = jnp.concatenate([wt, jnp.zeros((56, 256), BF)], axis=0)
        for c in range(4):
            g[pl.ds(8 * c, 8)] += nt(wobs[768 * c : 768 * c + 768, :], wt).reshape(8, 96, 128)

    g[:, 0:16, :] = jnp.zeros((32, 16, 128), F32)
    g[:, 80:96, :] = jnp.zeros((32, 16, 128), F32)

    bk[...] = jnp.zeros_like(bk)
    act[0:24] = jnp.zeros((24, 96, 384), BF)
    act[56:96] = jnp.zeros((40, 96, 384), BF)
    for c in range(4):
        x = g[8 * c : 8 * c + 8].reshape(768, 128).astype(BF)
        bk[16 + OFF + 8 * c : 24 + OFF + 8 * c, 8:104, :] = nn(x, dec_n[...]).reshape(8, 96, 128)

    @pl.loop(0, 4)
    def _(back):
        l = 3 - back
        d, reach = scal[l], scal[16 + l]
        first = 16 - reach + OFF

        @pl.loop(0, 16 + reach)
        def _(q):
            for u in range(2):
                i = first + 2 * q + u
                act[i, :, 0:128] = bk[i, pl.ds(8 - d, 96), :].astype(BF)
                act[i, :, 128:256] = bk[i, 8:104, :].astype(BF)
                act[i, :, 256:384] = bk[i, pl.ds(8 + d, 96), :].astype(BF)

        def store(rows, y):
            bk[rows, 8:104, :] += slope[l, rows].astype(F32) * y

        convolve(act, wb.at[l], d, first - d, 32 + 2 * (reach + d), store)

    if second:
        ga[:, 0:16, :] = jnp.zeros((32, 16, 128), F32)
        ga[:, 80:96, :] = jnp.zeros((32, 16, 128), F32)
        for f in range(8):
            base = 8 * scal[8 + f]
            inside = (base >= 16) & (base < 48)
            grow = jnp.where(inside, base - 16, 0)
            keep = jnp.where(inside, 1.0, 0.0)
            for r in range(8):
                x = bk[base + r + OFF, 8:104, :].astype(BF)
                y = (keep * (g[grow + r] + ga[grow + r])).astype(BF)
                x = jnp.concatenate([x, y], axis=1)
                edge = jnp.zeros((16, 256), BF)
                x = jnp.concatenate([edge, x, edge], axis=0)
                outs[f][r] = (-STEP * nt(enc_eye[...], x)).astype(BF)
    else:
        for half in range(2):
            for c in range(2):
                lo = 32 * half + 16 * c
                for sec in range(3):
                    x = bk[lo + OFF : lo + OFF + 16, 32 * sec + 8 : 32 * sec + 40, :].reshape(512, 128).astype(BF)
                    if half + c == 1:
                        y = g[lo - 16 : lo, 32 * sec : 32 * sec + 32, :].reshape(512, 128).astype(BF)
                        val = nt(enc_eye[...], jnp.concatenate([x, y], axis=1))
                    else:
                        val = nt(enc_eye[:, 0:128], x)
                    outs[half][:, 1024 * sec + 512 * c : 1024 * sec + 512 * c + 512] = val.astype(BF)
            rows = []
            for col in (32, 63):
                for i in range(32):
                    x = bk[32 * half + i + OFF, col + 8 : col + 9, :]
                    here = 32 * half + i - 16
                    if 0 <= here < 32:
                        y = g[here, col : col + 1, :]
                    else:
                        y = jnp.zeros((1, 128), F32)
                    rows.append(jnp.concatenate([x, y], axis=1))
            rows.append(jnp.zeros((64, 256), F32))
            x = jnp.concatenate(rows, axis=0).astype(BF)
            outs[half][:, 3072:3200] = nt(enc_eye[...], x).astype(BF)


def iteration(second, scal, count, *arrays):
    smem = pl.BlockSpec(memory_space=pltpu.SMEM)
    vmem = pl.BlockSpec(memory_space=pltpu.VMEM)
    if second:
        shapes = [jax.ShapeDtypeStruct((8, V, 128), BF)] * 8 + [jax.ShapeDtypeStruct((V, 4096), BF)]
    else:
        shapes = [jax.ShapeDtypeStruct((V, 3200), BF)] * 2
    return pl.pallas_call(
        functools.partial(iterate, second),
        out_shape=shapes,
        in_specs=[smem, smem] + [vmem] * len(arrays),
        out_specs=[vmem] * len(shapes),
        scratch_shapes=[
            pltpu.VMEM((64, 96, 128), F32),
            pltpu.VMEM((ROWS, 128, 128), F32),
            pltpu.VMEM((ROWS, 96, 384), BF),
            pltpu.VMEM((4, ROWS, 96, 128), BF),
            pltpu.VMEM((ROWS, 112, 128), F32),
            pltpu.VMEM((V, 3072), BF),
            pltpu.VMEM((3072, 256), BF),
            pltpu.VMEM((32, 96, 128), F32),
            pltpu.VMEM((32, 96, 128), F32),
            pltpu.VMEM((2, 112, 128), F32),
        ],
        compiler_params=pltpu.CompilerParams(vmem_limit_bytes=VMEM),
        cost_estimate=pl.CostEstimate(flops=10**10, bytes_accessed=6 * 10**6, transcendentals=3 * 10**6),
        name="second_iteration" if second else "first_iteration",
    )(scal, count, *arrays)


def paired(taps):
    none = jnp.zeros((taps.shape[0], 384, 128), BF)
    low, mid, top = taps[:, 0], taps[:, 1], taps[:, 2]
    first = jnp.concatenate([low, mid, top, none], axis=1)
    later = jnp.concatenate([none, low, mid, top], axis=1)
    return jnp.concatenate([first, later], axis=2)


def make_weights(encoder_weight, convolution_weight, decoder_weight):
    eye = jnp.eye(V, 128, dtype=BF)
    enc_v = jnp.pad(encoder_weight.T, ((0, 128 - 69), (0, 0)))
    dec_v = jnp.pad(decoder_weight, ((0, 128 - 69), (0, 0)))
    ahead = convolution_weight.transpose(0, 1, 3, 2).reshape(4, 3, 384, 128)
    back = convolution_weight[:, ::-1].reshape(4, 3, 384, 128)
    return (
        jnp.concatenate([enc_v[0:V], eye], axis=1),
        jnp.concatenate([dec_v[0:V], eye], axis=1),
        dec_v,
        paired(ahead),
        paired(back),
    )


def on_device(
    background,
    encoder_weight,
    convolution_weight,
    decoder_weight,
    dilations,
    obs_values,
    obs_prec,
    obs_frac,
    obs_dest,
    obs_cell,
    obs_count,
):
    smem = pl.BlockSpec(memory_space=pltpu.SMEM)
    vmem = pl.BlockSpec(memory_space=pltpu.VMEM)
    lon, lat = lax.axis_index("lon"), lax.axis_index("lat")
    sub = lon % 4
    flip = lat % 2 == 1

    def block_of(s):
        return jnp.where(flip, 3 - s, s)

    k = block_of(sub)
    top = 256 * lat + 64 * k
    came = [(sub - m) % 4 for m in range(4)]
    tables = [c + 2 for c in came] + [jnp.where(c >= 2, c - 2, c + 6) for c in came]
    d = dilations
    scal = jnp.stack(
        [d[0], d[1], d[2], d[3], 32 - top, 2048 + 32 - top, 64 * k, jnp.int32(0)]
        + tables
        + [d[1] + d[2] + d[3], d[2] + d[3], d[3], jnp.int32(0)]
        + [block_of((sub + m) % 4) for m in range(4)]
    ).astype(jnp.int32)

    cells = jnp.pad(background.astype(BF).transpose(1, 0, 2), ((0, 0), (0, V - 69), (0, 0)))
    before = lax.ppermute(cells[:, :, 224:256], AXES, BAND_UP)
    after = lax.ppermute(cells[:, :, 0:32], AXES, BAND_DOWN)
    sends = pl.pallas_call(
        split_kernel,
        out_shape=[jax.ShapeDtypeStruct((8, V, 128), BF)] * 4,
        in_specs=[smem] + [vmem] * 3,
        out_specs=[vmem] * 4,
        name="split",
    )(scal, cells, before, after)
    chunks = [sends[0]] + [lax.ppermute(sends[m % 4], AXES, family(m)) for m in range(1, 8)]

    rows = obs_dest.shape[0]
    alive = (jnp.arange(rows, dtype=jnp.int32) < obs_count[0]).astype(F32)
    packed, slots = pl.pallas_call(
        pack_kernel,
        out_shape=[jax.ShapeDtypeStruct((80, 1024), BF), jax.ShapeDtypeStruct((1, rows), jnp.int32)],
        in_specs=[vmem] * 5,
        out_specs=[vmem] * 2,
        name="pack",
    )(obs_values, (alive * obs_prec)[None, :], obs_frac, obs_dest.reshape(1, rows), obs_cell[None, :])
    pick = (slots.reshape(rows, 1) == jnp.arange(1024, dtype=jnp.int32)[None, :]).astype(BF)
    arrived = lax.all_to_all(packed, AXES, split_axis=1, concat_axis=1, tiled=True, axis_index_groups=GROUPS_32)
    others = [lax.ppermute(arrived, AXES, turn(m)) for m in range(1, 4)]
    comp, posx, count = pl.pallas_call(
        compact_kernel,
        out_shape=[
            jax.ShapeDtypeStruct((80, 4096), BF),
            jax.ShapeDtypeStruct((32, 128), F32),
            jax.ShapeDtypeStruct((1,), jnp.int32),
        ],
        in_specs=[smem] + [vmem] * 4,
        out_specs=[vmem, vmem, smem],
        scratch_shapes=[pltpu.VMEM((32, 128), F32)],
        name="compact",
    )(scal, arrived, *others)

    weights = make_weights(encoder_weight, convolution_weight, decoder_weight)

    left, right = iteration(False, scal, count, *chunks, *weights, comp)
    left_in = lax.ppermute(right, AXES, LON_UP)
    right_in = lax.ppermute(left, AXES, LON_DOWN)
    left = (left.astype(F32) + left_in.astype(F32)).astype(BF)
    right = (right.astype(F32) + right_in.astype(F32)).astype(BF)
    extra = [left[:, 3072:3200], right[:, 3072:3200]]
    from_next = lax.ppermute(jnp.concatenate([left[:, 0:1024], right[:, 0:1024]] + extra, axis=1), AXES, LAT_DOWN)
    from_prev = lax.ppermute(jnp.concatenate([left[:, 2048:3072], right[:, 2048:3072]] + extra, axis=1), AXES, LAT_UP)
    *moves, found = iteration(True, scal, count, *chunks, *weights, comp, left, right, from_prev, from_next)

    spread = pl.pallas_call(
        expand_kernel,
        out_shape=[jax.ShapeDtypeStruct((V, 1024), BF)] * 4,
        in_specs=[smem, vmem, vmem],
        out_specs=[vmem] * 4,
        scratch_shapes=[pltpu.VMEM((V, 4096), F32)],
        name="expand",
    )(count, posx, found)
    moves = lax.optimization_barrier((*moves, *spread))
    moves, spread = moves[0:8], moves[8:12]
    parts = [lax.ppermute(spread[m], AXES, turn(m)) for m in range(1, 4)]
    parts = [p.astype(F32) for p in [spread[0]] + parts]
    spread = (parts[0] + parts[1] + parts[2] + parts[3]).astype(BF)
    spread = lax.all_to_all(spread, AXES, split_axis=1, concat_axis=1, tiled=True, axis_index_groups=GROUPS_32)
    equivalent = jnp.einsum("vs,rs->vr", spread[0:69], pick, preferred_element_type=F32)
    innovation = alive[None, :] * (equivalent - obs_values)

    back = [moves[0]] + [lax.ppermute(moves[m], AXES, [(b, a) for a, b in family(m)]) for m in range(1, 8)]
    total = jnp.zeros((8, V, 320), F32)
    summed = jnp.stack([back[m].astype(F32) + back[m + 4].astype(F32) for m in range(4)])
    for b in range(4):
        m = (jnp.where(flip, 3 - b, b) - sub) % 4
        block = lax.dynamic_index_in_dim(summed, m, 0, keepdims=False)
        total = total + jnp.pad(block, ((0, 0), (0, 0), (64 * b, 192 - 64 * b)))
    edge_up = lax.ppermute(total[:, :, 288:320].astype(BF), AXES, BAND_UP)
    edge_down = lax.ppermute(total[:, :, 0:32].astype(BF), AXES, BAND_DOWN)
    total = total[:, :, 32:288]
    total = total + jnp.pad(edge_up.astype(F32), ((0, 0), (0, 0), (0, 224)))
    total = total + jnp.pad(edge_down.astype(F32), ((0, 0), (0, 0), (224, 0)))
    analysis = background + total[:, 0:69, :].transpose(1, 0, 2)
    return (analysis, innovation)


def solution(mesh):
    placed = (
        P(None, "lon", "lat"),
        P(),
        P(),
        P(),
        P(),
        P(None, ("lon", "lat")),
        P(("lon", "lat")),
        P(None, ("lon", "lat")),
        P(("lon", "lat"), None),
        P(("lon", "lat")),
        P(("lon", "lat")),
    )
    return jax.shard_map(
        on_device,
        mesh=mesh,
        in_specs=placed,
        out_specs=(P(None, "lon", "lat"), P(None, ("lon", "lat"))),
        check_vma=False,
    )
```

```python
import functools

import jax
import jax.numpy as jnp
from jax import lax
from jax.experimental import pallas as pl
from jax.experimental.pallas import tpu as pltpu
from jax.sharding import PartitionSpec as P

AXES = ("lon", "lat")
BF = jnp.bfloat16
F32 = jnp.float32
V = 72
OFF = 8
ROWS = 96
R = 16
STEP = 0.25
VMEM = 60 * 1024 * 1024


def snake(s, lat):
    return s if lat % 2 == 0 else 3 - s


def device(lon, lat):
    return 8 * lon + lat


def worker(y, p):
    lat, k = p // 4, p % 4
    return device(4 * y + snake(k, lat), lat)


LON_UP = [(worker(y, p), worker((y + 1) % 4, p)) for y in range(4) for p in range(32)]
LON_DOWN = [(b, a) for a, b in LON_UP]
LAT_UP = [(worker(y, p), worker(y, p + 1)) for y in range(4) for p in range(31)]
LAT_DOWN = [(b, a) for a, b in LAT_UP]
BAND_UP = [(device(n, l), device(n, l + 1)) for n in range(16) for l in range(7)]
BAND_DOWN = [(b, a) for a, b in BAND_UP]
GROUPS_32 = [[device(4 * y + s, l) for y in range(4) for l in range(8)] for s in range(4)]
GROUPS_4 = [[device(4 * y + s, l) for s in range(4)] for y in range(4) for l in range(8)]


def family(m):
    return [(g[s], g[(s + m) % 4]) for g in GROUPS_4 for s in range(4)]


def swap(x):
    return [(g[s], g[s ^ x]) for g in GROUPS_4 for s in range(4)]


def nt(a, b):
    return lax.dot_general(a, b, (((1,), (1,)), ((), ())), preferred_element_type=F32)


def tn(a, b):
    return lax.dot_general(a, b, (((0,), (0,)), ((), ())), preferred_element_type=F32)


def nn(a, b):
    return jnp.dot(a, b, preferred_element_type=F32)


def pack_kernel(values, prec, frac, dest, cell, packed, slots):
    rows = dest.shape[1]
    owner = dest[...]
    group = lax.shift_right_logical(owner, 5) * 8 + (owner & 7)
    member = lax.broadcasted_iota(jnp.int32, (32, rows), 0) == group
    row = lax.broadcasted_iota(jnp.int32, (rows, rows), 0)
    col = lax.broadcasted_iota(jnp.int32, (rows, rows), 1)
    before = nn(jnp.where(member, 1.0, 0.0).astype(BF), jnp.where(row < col, 1.0, 0.0).astype(BF))
    rank = jnp.sum(jnp.where(member, before, 0.0), axis=0, keepdims=True)
    slot = group * 32 + rank.astype(jnp.int32)
    slots[...] = slot
    lon = jnp.zeros((1, rows), F32)
    code = cell[...]
    for step in range(1, 7):
        lon = lon + jnp.where(code >= 255 * step, 1.0, 0.0)
    lat = code.astype(F32) - 255.0 * lon
    lon = lon + 8.0 * (lax.shift_right_logical(owner, 3) & 3).astype(F32)
    parts = []
    for x in (prec[...], frac[0:1], frac[1:2]):
        high = x.astype(BF).astype(F32)
        parts += [high, x - high]
    ctrl = jnp.concatenate(parts + [lon, lat], axis=0)
    payload = jnp.concatenate([values[...], jnp.zeros((3, rows), F32), ctrl], axis=0).astype(BF)
    for c in range(4):
        index = lax.broadcasted_iota(jnp.int32, (256, rows), 0) + 256 * c
        pick = jnp.where(index == slot, 1.0, 0.0).astype(BF)
        packed[:, 256 * c : 256 * c + 256] = nt(payload, pick).astype(BF)


def split_kernel(scal, cells, before, after, *outs):
    for b in range(4):
        for m in range(4):
            @pl.when(scal[20 + m] == b)
            def _():
                for r in range(8):
                    if b == 0:
                        x = jnp.concatenate([before[r], cells[r, :, 0:96]], axis=1)
                    elif b == 3:
                        x = jnp.concatenate([cells[r, :, 160:256], after[r]], axis=1)
                    else:
                        x = cells[r, :, 64 * b - 32 : 64 * b + 96]
                    outs[m][r] = x


def order_kernel(scal, *refs):
    chunks, outs = refs[0:4], refs[4:6]
    for m in range(4):
        for c in range(4):
            @pl.when(scal[8 + m] == c)
            def _():
                outs[c // 2][8 * (c % 2) : 8 * (c % 2) + 8] = chunks[m][...]


def gather_kernel(scal, low, low_in, high, high_in, *outs):
    for m in range(4):
        for c in range(4):
            @pl.when(scal[8 + m] == c)
            def _():
                rows = pl.ds(8 * (c % 2), 8)
                x, y = (low, low_in) if c < 2 else (high, high_in)
                outs[m][...] = (x[rows].astype(F32) + y[rows].astype(F32)).astype(BF)


def compact_kernel(scal, pay0, pay1, pay2, pay3, comp, posx, count, total):
    pays = (pay0, pay1, pay2, pay3)
    k64 = scal[6].astype(F32)
    mine, own = [], []
    for part in range(4):
        ctrl = pays[part][...].astype(F32)[72:80]
        local = ctrl[7:8] - k64
        live = ctrl[0:1] > 0.0
        mine.append(jnp.where(live & (local >= -1.0) & (local <= 63.0), 1.0, 0.0))
        own.append(jnp.where(live & (local >= 0.0) & (local <= 63.0), 1.0, 0.0))
    mine = jnp.concatenate([m[:, 128 * c : 128 * c + 128] for m in mine for c in range(8)], axis=0)
    own = jnp.concatenate([m[:, 128 * c : 128 * c + 128] for m in own for c in range(8)], axis=0)
    row = lax.broadcasted_iota(jnp.int32, (128, 128), 0)
    col = lax.broadcasted_iota(jnp.int32, (128, 128), 1)
    before = nn(mine.astype(BF), jnp.where(row < col, 1.0, 0.0).astype(BF))
    sums = nn(mine.astype(BF), jnp.ones((128, 128), BF))
    row4 = lax.broadcasted_iota(jnp.int32, (32, 32), 0)
    col4 = lax.broadcasted_iota(jnp.int32, (32, 32), 1)
    offset = nn(jnp.where(col4 < row4, 1.0, 0.0).astype(BF), sums.astype(BF))
    place = before + offset
    owned = jnp.where(own > 0.0, place, -1.0)
    posx[...] = owned
    total[...] = jnp.where(mine > 0.0, place, -1.0)
    number = jnp.sum(mine).astype(jnp.int32)
    count[0] = number
    comp[...] = jnp.zeros_like(comp)
    index = lax.broadcasted_iota(jnp.int32, (256, 128), 0).astype(F32)

    @pl.loop(0, (number + 255) // 256)
    def _(tile):
        ids = index + (tile * 256).astype(F32)
        out = jnp.zeros((80, 256), F32)
        for c in range(0, 32, 2):
            picks = jnp.concatenate(
                [jnp.where(ids == total[c + h : c + h + 1, :], 1.0, 0.0).astype(BF) for h in (0, 1)], axis=1
            )
            out = out + nt(pays[c // 8][:, 128 * (c % 8) : 128 * (c % 8) + 256], picks)
        comp[:, pl.ds(pl.multiple_of(tile * 256, 256), 256)] = out.astype(BF)


def expand_kernel(count, posx, found, *refs):
    outs, total = refs[0:4], refs[4]
    index = lax.broadcasted_iota(jnp.int32, (256, 128), 0).astype(F32)
    total[...] = jnp.zeros_like(total)

    @pl.loop(0, (count[0] + 255) // 256)
    def _(tile):
        ids = index + (tile * 256).astype(F32)
        rows = found[:, pl.ds(pl.multiple_of(tile * 256, 256), 256)]
        for c in range(32):
            picks = jnp.where(ids == posx[c : c + 1, :], 1.0, 0.0).astype(BF)
            total[:, 128 * c : 128 * c + 128] += nn(rows, picks)

    for m in range(4):
        outs[m][...] = total[:, 1024 * m : 1024 * m + 1024].astype(BF)


def convolve(act, weight, d, first, count, store):
    for dd in range(1, 5):
        blocks = 8 // dd
        step = 2 * blocks * dd

        @pl.when(d == dd)
        def _():
            @pl.loop(0, (count + step - 1) // step)
            def _(c):
                i = first + step * c
                x = act[pl.ds(i - dd, step + 2 * dd)].reshape(blocks + 1, 2, dd, 96, 384)
                m = blocks * dd * 96
                x = [x[p // 2 : p // 2 + blocks, p % 2].reshape(m, 384) for p in range(4)]
                y = nn(jnp.concatenate(x, axis=1), weight[...])
                y = jnp.stack([y[:, 128 * p : 128 * p + 128].reshape(blocks, dd, 96, 128) for p in (0, 1)], axis=1)
                store(pl.ds(i, step), y.reshape(step, 96, 128))


def iterate(second, *refs):
    scal, count = refs[0:2]
    chunks = refs[2:6]
    enc_eye, dec_eye, dec_n, wf, wb, comp = refs[6:12]
    refs = refs[12:]
    if second:
        tots, from_prev, from_next = refs[0:2], refs[2], refs[3]
        outs, found = refs[4:8], refs[8]
        refs = refs[9:]
    else:
        outs = refs[0:2]
        refs = refs[2:]
    st, h, act, slope, bk, fct, wobs, g, ga, shift = refs

    act[60:96] = jnp.zeros((36, 96, 384), BF)

    for i in range(64):
        chunk = chunks[i // 16][i % 16]
        if 16 <= i < 48:
            both = tn(chunk, enc_eye[...])
            st[i - 16] = both[16:112, 128:256]
        else:
            both = tn(chunk, enc_eye[:, 0:128])
        h[i + OFF] = both[:, 0:128]
    if second:
        for half in range(2):
            tot = tots[half]
            for c in range(2):
                row = 32 * half + 16 * c
                lanes = 1024 * half + 512 * c
                for sec in range(3):
                    add = tot[:, 1024 * sec + 512 * c : 1024 * sec + 512 * c + 512].astype(F32)
                    if sec == 0:
                        add = add + from_prev[:, lanes : lanes + 512].astype(F32)
                    if sec == 2:
                        add = add + from_next[:, lanes : lanes + 512].astype(F32)
                    both = tn(add.astype(BF), enc_eye[...]).reshape(16, 32, 256)
                    h[row + OFF : row + OFF + 16, 16 + 32 * sec : 48 + 32 * sec, :] -= STEP * both[:, :, 0:128]
                    if half + c == 1:
                        st[row - 16 : row, 32 * sec : 32 + 32 * sec, :] -= STEP * both[:, :, 128:256]
                        ga[row - 16 : row, 32 * sec : 32 * sec + 32, :] = 0.75 * both[:, :, 128:256]
            low = tn(from_prev[:, 2048 + 128 * half : 2176 + 128 * half], enc_eye[:, 0:128])
            high = tn(from_next[:, 2048 + 128 * half : 2176 + 128 * half], enc_eye[:, 0:128])
            for i in range(32):
                h[32 * half + i + OFF, 15:16, :] -= STEP * low[32 + i : 33 + i]
                h[32 * half + i + OFF, 112:113, :] -= STEP * high[i : i + 1]

    e = lax.broadcasted_iota(jnp.int32, (112, 128), 0) + 8
    mask = jnp.where((e >= scal[4]) & (e < scal[5]), 1.0, 0.0)

    @pl.loop(0, 4)
    def _(l):
        d, reach = scal[l], scal[16 + l]
        first = 16 - reach - d + OFF

        @pl.loop(0, 16 + reach + d)
        def _(q):
            for u in range(2):
                i = first + 2 * q + u
                t = jnp.tanh(h[i, 8:120, :])
                slope[l, i] = ((1.0 - t * t) * mask)[8:104].astype(BF)
                t = t * mask
                shift[u] = t
                act[i, :, 0:128] = shift[u, pl.ds(8 - d, 96), :].astype(BF)
                act[i, :, 128:256] = t[8:104].astype(BF)
                act[i, :, 256:384] = shift[u, pl.ds(8 + d, 96), :].astype(BF)

        for u in range(R):
            slope[l, 48 + reach + d + OFF + u] = jnp.zeros((96, 128), BF)

        def store(rows, y):
            h[rows, 16:112, :] += y

        convolve(act, wf.at[l], d, 16 - reach + OFF, 32 + 2 * reach, store)

    for c in range(4):
        a = h[16 + OFF + 8 * c : 24 + OFF + 8 * c, 16:112, :].reshape(768, 128).astype(BF)
        b = st[8 * c : 8 + 8 * c].reshape(768, 128).astype(BF)
        fct[:, 768 * c : 768 * c + 768] = nt(dec_eye[...], jnp.concatenate([a, b], axis=1)).astype(BF)

    g[...] = jnp.zeros_like(g)
    k64 = scal[6].astype(F32)
    lon_of = lax.broadcasted_iota(jnp.int32, (32, 256), 0).astype(F32)
    lat_of = lax.broadcasted_iota(jnp.int32, (96, 256), 0).astype(F32) - 16.0

    @pl.loop(0, (count[0] + 255) // 256)
    def _(tile):
        lanes = pl.ds(pl.multiple_of(tile * 256, 256), 256)
        pay = comp[:, lanes].astype(F32)
        prec = pay[72:73] + pay[73:74]
        fu = pay[74:75] + pay[75:76]
        fv = pay[76:77] + pay[77:78]
        li, lj = pay[78:79], pay[79:80] - k64
        wa = jnp.where(lon_of == li, 1.0 - fu, 0.0) + jnp.where(lon_of == li + 1.0, fu, 0.0)
        wl = (jnp.where(lat_of == lj, 1.0 - fv, 0.0) + jnp.where(lat_of == lj + 1.0, fv, 0.0)).astype(BF)
        wa = wa.astype(BF)
        for i in range(32):
            wobs[96 * i : 96 * i + 96, :] = wa[i : i + 1] * wl
        eq = nn(fct[...], wobs[...])
        if second:
            found[:, lanes] = eq.astype(BF)
        wt = (prec * (eq - pay[0:72])).astype(BF)
        wt = jnp.concatenate([wt, jnp.zeros((56, 256), BF)], axis=0)
        for c in range(4):
            g[pl.ds(8 * c, 8)] += nt(wobs[768 * c : 768 * c + 768, :], wt).reshape(8, 96, 128)

    g[:, 0:16, :] = jnp.zeros((32, 16, 128), F32)
    g[:, 80:96, :] = jnp.zeros((32, 16, 128), F32)

    bk[...] = jnp.zeros_like(bk)
    act[0:24] = jnp.zeros((24, 96, 384), BF)
    act[56:96] = jnp.zeros((40, 96, 384), BF)
    for c in range(4):
        x = g[8 * c : 8 * c + 8].reshape(768, 128).astype(BF)
        bk[16 + OFF + 8 * c : 24 + OFF + 8 * c, 8:104, :] = nn(x, dec_n[...]).reshape(8, 96, 128)

    @pl.loop(0, 4)
    def _(back):
        l = 3 - back
        d, reach = scal[l], scal[16 + l]
        first = 16 - reach + OFF

        @pl.loop(0, 16 + reach)
        def _(q):
            for u in range(2):
                i = first + 2 * q + u
                act[i, :, 0:128] = bk[i, pl.ds(8 - d, 96), :].astype(BF)
                act[i, :, 128:256] = bk[i, 8:104, :].astype(BF)
                act[i, :, 256:384] = bk[i, pl.ds(8 + d, 96), :].astype(BF)

        def store(rows, y):
            bk[rows, 8:104, :] += slope[l, rows].astype(F32) * y

        convolve(act, wb.at[l], d, first - d, 32 + 2 * (reach + d), store)

    if second:
        ga[:, 0:16, :] = jnp.zeros((32, 16, 128), F32)
        ga[:, 80:96, :] = jnp.zeros((32, 16, 128), F32)
        edge = jnp.zeros((16, 128), BF)
        for i in range(64):
            x = jnp.concatenate([edge, bk[i + OFF, 8:104, :].astype(BF), edge], axis=0)
            if 16 <= i < 48:
                y = (g[i - 16] + ga[i - 16]).astype(BF)
                y = jnp.concatenate([edge, y, edge], axis=0)
                val = nt(enc_eye[...], jnp.concatenate([x, y], axis=1))
            else:
                val = nt(enc_eye[:, 0:128], x)
            outs[i // 16][i % 16] = (-STEP * val).astype(BF)
    else:
        for half in range(2):
            for c in range(2):
                lo = 32 * half + 16 * c
                for sec in range(3):
                    x = bk[lo + OFF : lo + OFF + 16, 32 * sec + 8 : 32 * sec + 40, :].reshape(512, 128).astype(BF)
                    if half + c == 1:
                        y = g[lo - 16 : lo, 32 * sec : 32 * sec + 32, :].reshape(512, 128).astype(BF)
                        val = nt(enc_eye[...], jnp.concatenate([x, y], axis=1))
                    else:
                        val = nt(enc_eye[:, 0:128], x)
                    outs[half][:, 1024 * sec + 512 * c : 1024 * sec + 512 * c + 512] = val.astype(BF)
            rows = []
            for col in (32, 63):
                for i in range(32):
                    x = bk[32 * half + i + OFF, col + 8 : col + 9, :]
                    here = 32 * half + i - 16
                    if 0 <= here < 32:
                        y = g[here, col : col + 1, :]
                    else:
                        y = jnp.zeros((1, 128), F32)
                    rows.append(jnp.concatenate([x, y], axis=1))
            rows.append(jnp.zeros((64, 256), F32))
            x = jnp.concatenate(rows, axis=0).astype(BF)
            outs[half][:, 3072:3200] = nt(enc_eye[...], x).astype(BF)


def iteration(second, scal, count, *arrays):
    smem = pl.BlockSpec(memory_space=pltpu.SMEM)
    vmem = pl.BlockSpec(memory_space=pltpu.VMEM)
    if second:
        shapes = [jax.ShapeDtypeStruct((16, V, 128), BF)] * 4 + [jax.ShapeDtypeStruct((V, 4096), BF)]
    else:
        shapes = [jax.ShapeDtypeStruct((V, 3200), BF)] * 2
    return pl.pallas_call(
        functools.partial(iterate, second),
        out_shape=shapes,
        in_specs=[smem, smem] + [vmem] * len(arrays),
        out_specs=[vmem] * len(shapes),
        scratch_shapes=[
            pltpu.VMEM((32, 96, 128), F32),
            pltpu.VMEM((ROWS, 128, 128), F32),
            pltpu.VMEM((ROWS, 96, 384), BF),
            pltpu.VMEM((4, ROWS, 96, 128), BF),
            pltpu.VMEM((ROWS, 112, 128), F32),
            pltpu.VMEM((V, 3072), BF),
            pltpu.VMEM((3072, 256), BF),
            pltpu.VMEM((32, 96, 128), F32),
            pltpu.VMEM((32, 96, 128), F32),
            pltpu.VMEM((2, 112, 128), F32),
        ],
        compiler_params=pltpu.CompilerParams(vmem_limit_bytes=VMEM),
        cost_estimate=pl.CostEstimate(flops=10**10, bytes_accessed=6 * 10**6, transcendentals=3 * 10**6),
        name="second_iteration" if second else "first_iteration",
    )(scal, count, *arrays)


def paired(taps):
    none = jnp.zeros((taps.shape[0], 384, 128), BF)
    low, mid, top = taps[:, 0], taps[:, 1], taps[:, 2]
    first = jnp.concatenate([low, mid, top, none], axis=1)
    later = jnp.concatenate([none, low, mid, top], axis=1)
    return jnp.concatenate([first, later], axis=2)


def make_weights(encoder_weight, convolution_weight, decoder_weight):
    eye = jnp.eye(V, 128, dtype=BF)
    enc_v = jnp.pad(encoder_weight.T, ((0, 128 - 69), (0, 0)))
    dec_v = jnp.pad(decoder_weight, ((0, 128 - 69), (0, 0)))
    ahead = convolution_weight.transpose(0, 1, 3, 2).reshape(4, 3, 384, 128)
    back = convolution_weight[:, ::-1].reshape(4, 3, 384, 128)
    return (
        jnp.concatenate([enc_v[0:V], eye], axis=1),
        jnp.concatenate([dec_v[0:V], eye], axis=1),
        dec_v,
        paired(ahead),
        paired(back),
    )


def on_device(
    background,
    encoder_weight,
    convolution_weight,
    decoder_weight,
    dilations,
    obs_values,
    obs_prec,
    obs_frac,
    obs_dest,
    obs_cell,
    obs_count,
):
    smem = pl.BlockSpec(memory_space=pltpu.SMEM)
    vmem = pl.BlockSpec(memory_space=pltpu.VMEM)
    lon, lat = lax.axis_index("lon"), lax.axis_index("lat")
    sub = lon % 4
    flip = lat % 2 == 1

    def block_of(s):
        return jnp.where(flip, 3 - s, s)

    k = block_of(sub)
    top = 256 * lat + 64 * k
    came = [(sub - m) % 4 for m in range(4)]
    tables = came + [jnp.int32(0)] * 4
    d = dilations
    scal = jnp.stack(
        [d[0], d[1], d[2], d[3], 32 - top, 2048 + 32 - top, 64 * k, jnp.int32(0)]
        + tables
        + [d[1] + d[2] + d[3], d[2] + d[3], d[3], jnp.int32(0)]
        + [block_of((sub + m) % 4) for m in range(4)]
    ).astype(jnp.int32)

    cells = jnp.pad(background.astype(BF).transpose(1, 0, 2), ((0, 0), (0, V - 69), (0, 0)))
    before = lax.ppermute(cells[:, :, 224:256], AXES, BAND_UP)
    after = lax.ppermute(cells[:, :, 0:32], AXES, BAND_DOWN)
    sends = pl.pallas_call(
        split_kernel,
        out_shape=[jax.ShapeDtypeStruct((8, V, 128), BF)] * 4,
        in_specs=[smem] + [vmem] * 3,
        out_specs=[vmem] * 4,
        name="split",
    )(scal, cells, before, after)
    chunks = [sends[0]] + [lax.ppermute(sends[m], AXES, family(m)) for m in range(1, 4)]
    low, high = pl.pallas_call(
        order_kernel,
        out_shape=[jax.ShapeDtypeStruct((16, V, 128), BF)] * 2,
        in_specs=[smem] + [vmem] * 4,
        out_specs=[vmem] * 2,
        name="order",
    )(scal, *chunks)
    chunks = [lax.ppermute(high, AXES, LON_UP), low, high, lax.ppermute(low, AXES, LON_DOWN)]

    rows = obs_dest.shape[0]
    alive = (jnp.arange(rows, dtype=jnp.int32) < obs_count[0]).astype(F32)
    packed, slots = pl.pallas_call(
        pack_kernel,
        out_shape=[jax.ShapeDtypeStruct((80, 1024), BF), jax.ShapeDtypeStruct((1, rows), jnp.int32)],
        in_specs=[vmem] * 5,
        out_specs=[vmem] * 2,
        name="pack",
    )(obs_values, (alive * obs_prec)[None, :], obs_frac, obs_dest.reshape(1, rows), obs_cell[None, :])
    pick = (slots.reshape(rows, 1) == jnp.arange(1024, dtype=jnp.int32)[None, :]).astype(BF)
    arrived = lax.all_to_all(packed, AXES, split_axis=1, concat_axis=1, tiled=True, axis_index_groups=GROUPS_32)
    across = lax.ppermute(arrived, AXES, swap(2))
    others = [lax.ppermute(arrived, AXES, swap(1)), across, lax.ppermute(across, AXES, swap(1))]
    comp, posx, count = pl.pallas_call(
        compact_kernel,
        out_shape=[
            jax.ShapeDtypeStruct((80, 4096), BF),
            jax.ShapeDtypeStruct((32, 128), F32),
            jax.ShapeDtypeStruct((1,), jnp.int32),
        ],
        in_specs=[smem] + [vmem] * 4,
        out_specs=[vmem, vmem, smem],
        scratch_shapes=[pltpu.VMEM((32, 128), F32)],
        name="compact",
    )(scal, arrived, *others)

    weights = make_weights(encoder_weight, convolution_weight, decoder_weight)

    left, right = iteration(False, scal, count, *chunks, *weights, comp)
    left_in = lax.ppermute(right, AXES, LON_UP)
    right_in = lax.ppermute(left, AXES, LON_DOWN)
    left = (left.astype(F32) + left_in.astype(F32)).astype(BF)
    right = (right.astype(F32) + right_in.astype(F32)).astype(BF)
    extra = [left[:, 3072:3200], right[:, 3072:3200]]
    from_next = lax.ppermute(jnp.concatenate([left[:, 0:1024], right[:, 0:1024]] + extra, axis=1), AXES, LAT_DOWN)
    from_prev = lax.ppermute(jnp.concatenate([left[:, 2048:3072], right[:, 2048:3072]] + extra, axis=1), AXES, LAT_UP)
    *moves, found = iteration(True, scal, count, *chunks, *weights, comp, left, right, from_prev, from_next)

    low_in = lax.ppermute(moves[3], AXES, LON_UP)
    high_in = lax.ppermute(moves[0], AXES, LON_DOWN)

    spread = pl.pallas_call(
        expand_kernel,
        out_shape=[jax.ShapeDtypeStruct((V, 1024), BF)] * 4,
        in_specs=[smem, vmem, vmem],
        out_specs=[vmem] * 4,
        scratch_shapes=[pltpu.VMEM((V, 4096), F32)],
        name="expand",
    )(count, posx, found)
    parts = [lax.ppermute(spread[m], AXES, swap(m)) for m in range(1, 4)]
    parts = [p.astype(F32) for p in [spread[0]] + parts]
    spread = (parts[0] + parts[1] + parts[2] + parts[3]).astype(BF)
    spread = lax.all_to_all(spread, AXES, split_axis=1, concat_axis=1, tiled=True, axis_index_groups=GROUPS_32)
    equivalent = jnp.einsum("vs,rs->vr", spread[0:69], pick, preferred_element_type=F32)
    innovation = alive[None, :] * (equivalent - obs_values)

    moves = pl.pallas_call(
        gather_kernel,
        out_shape=[jax.ShapeDtypeStruct((8, V, 128), BF)] * 4,
        in_specs=[smem] + [vmem] * 4,
        out_specs=[vmem] * 4,
        name="gather",
    )(scal, moves[1], low_in, moves[2], high_in)
    back = [moves[0]] + [lax.ppermute(moves[m], AXES, [(b, a) for a, b in family(m)]) for m in range(1, 4)]
    total = jnp.zeros((8, V, 320), F32)
    summed = jnp.stack(back).astype(F32)
    for b in range(4):
        m = (jnp.where(flip, 3 - b, b) - sub) % 4
        block = lax.dynamic_index_in_dim(summed, m, 0, keepdims=False)
        total = total + jnp.pad(block, ((0, 0), (0, 0), (64 * b, 192 - 64 * b)))
    edge_up = lax.ppermute(total[:, :, 288:320].astype(BF), AXES, BAND_UP)
    edge_down = lax.ppermute(total[:, :, 0:32].astype(BF), AXES, BAND_DOWN)
    total = total[:, :, 32:288]
    total = total + jnp.pad(edge_up.astype(F32), ((0, 0), (0, 0), (0, 224)))
    total = total + jnp.pad(edge_down.astype(F32), ((0, 0), (0, 0), (224, 0)))
    analysis = background + total[:, 0:69, :].transpose(1, 0, 2)
    return (analysis, innovation)


def solution(mesh):
    placed = (
        P(None, "lon", "lat"),
        P(),
        P(),
        P(),
        P(),
        P(None, ("lon", "lat")),
        P(("lon", "lat")),
        P(None, ("lon", "lat")),
        P(("lon", "lat"), None),
        P(("lon", "lat")),
        P(("lon", "lat")),
    )
    return jax.shard_map(
        on_device,
        mesh=mesh,
        in_specs=placed,
        out_specs=(P(None, "lon", "lat"), P(None, ("lon", "lat"))),
        check_vma=False,
    )
```

```python
import functools

import jax
import jax.numpy as jnp
import numpy as np
from jax import lax
from jax.experimental import pallas as pl
from jax.experimental.pallas import tpu as pltpu
from jax.sharding import PartitionSpec as P

AXES = ("lon", "lat")
BF = jnp.bfloat16
F32 = jnp.float32
V = 72
OFF = 8
ROWS = 96
R = 16
STEP = 0.25
VMEM = 60 * 1024 * 1024


def snake(s, lat):
    return s if lat % 2 == 0 else 3 - s


def device(lon, lat):
    return 8 * lon + lat


def worker(y, p):
    lat, k = p // 4, p % 4
    return device(4 * y + snake(k, lat), lat)


LON_UP = [(worker(y, p), worker((y + 1) % 4, p)) for y in range(4) for p in range(32)]
LON_DOWN = [(b, a) for a, b in LON_UP]
LAT_UP = [(worker(y, p), worker(y, p + 1)) for y in range(4) for p in range(31)]
LAT_DOWN = [(b, a) for a, b in LAT_UP]
BAND_UP = [(device(n, l), device(n, l + 1)) for n in range(16) for l in range(7)]
BAND_DOWN = [(b, a) for a, b in BAND_UP]
GROUPS_32 = [[device(4 * y + s, l) for y in range(4) for l in range(8)] for s in range(4)]
GROUPS_4 = [[device(4 * y + s, l) for s in range(4)] for y in range(4) for l in range(8)]


def family(m):
    return [(g[s], g[(s + m) % 4]) for g in GROUPS_4 for s in range(4)]


def places():
    table = np.zeros((128, 12), np.int32)
    for n in range(16):
        for l in range(8):
            k = snake(n % 4, l)
            top = 256 * l + 64 * k
            table[8 * n + l, 0:3] = (32 - top, 2048 + 32 - top, 64 * k)
            for m in range(4):
                table[8 * n + l, 4 + m] = (n % 4 - m) % 4
                table[8 * n + l, 8 + m] = snake((n % 4 + m) % 4, l)
    return table


PLACES = places()


def reach_after(scal, l):
    return sum(jnp.where(l < n, scal[n], 0) for n in (1, 2, 3))


def swap(x):
    return [(g[s], g[s ^ x]) for g in GROUPS_4 for s in range(4)]


def nt(a, b):
    return lax.dot_general(a, b, (((1,), (1,)), ((), ())), preferred_element_type=F32)


def tn(a, b):
    return lax.dot_general(a, b, (((0,), (0,)), ((), ())), preferred_element_type=F32)


def nn(a, b):
    return jnp.dot(a, b, preferred_element_type=F32)


def pack_kernel(values, prec, frac, dest, cell, packed, slots):
    rows = dest.shape[1]
    owner = dest[...]
    group = lax.shift_right_logical(owner, 5) * 8 + (owner & 7)
    member = lax.broadcasted_iota(jnp.int32, (32, rows), 0) == group
    row = lax.broadcasted_iota(jnp.int32, (rows, rows), 0)
    col = lax.broadcasted_iota(jnp.int32, (rows, rows), 1)
    before = nn(jnp.where(member, 1.0, 0.0).astype(BF), jnp.where(row < col, 1.0, 0.0).astype(BF))
    rank = jnp.sum(jnp.where(member, before, 0.0), axis=0, keepdims=True)
    slot = group * 32 + rank.astype(jnp.int32)
    slots[...] = slot
    lon = jnp.zeros((1, rows), F32)
    code = cell[...]
    for step in range(1, 7):
        lon = lon + jnp.where(code >= 255 * step, 1.0, 0.0)
    lat = code.astype(F32) - 255.0 * lon
    lon = lon + 8.0 * (lax.shift_right_logical(owner, 3) & 3).astype(F32)
    parts = []
    for x in (prec[...], frac[0:1], frac[1:2]):
        high = x.astype(BF).astype(F32)
        parts += [high, x - high]
    ctrl = jnp.concatenate(parts + [lon, lat], axis=0)
    payload = jnp.concatenate([values[...], jnp.zeros((3, rows), F32), ctrl], axis=0).astype(BF)
    for c in range(4):
        index = lax.broadcasted_iota(jnp.int32, (256, rows), 0) + 256 * c
        pick = jnp.where(index == slot, 1.0, 0.0).astype(BF)
        packed[:, 256 * c : 256 * c + 256] = nt(payload, pick).astype(BF)


def split_kernel(scal, cells, before, after, *outs):
    for b in range(4):
        for m in range(4):
            @pl.when(scal[12 + m] == b)
            def _():
                for r in range(8):
                    if b == 0:
                        x = jnp.concatenate([before[r], cells[r, :, 0:96]], axis=1)
                    elif b == 3:
                        x = jnp.concatenate([cells[r, :, 160:256], after[r]], axis=1)
                    else:
                        x = cells[r, :, 64 * b - 32 : 64 * b + 96]
                    outs[m][r] = x


def order_kernel(scal, *refs):
    chunks, outs = refs[0:4], refs[4:6]
    for m in range(4):
        for c in range(4):
            @pl.when(scal[8 + m] == c)
            def _():
                outs[c // 2][8 * (c % 2) : 8 * (c % 2) + 8] = chunks[m][...]


def gather_kernel(scal, low, low_in, high, high_in, *outs):
    for m in range(4):
        for c in range(4):
            @pl.when(scal[8 + m] == c)
            def _():
                rows = pl.ds(8 * (c % 2), 8)
                x, y = (low, low_in) if c < 2 else (high, high_in)
                outs[m][...] = (x[rows].astype(F32) + y[rows].astype(F32)).astype(BF)


def compact_kernel(scal, pay0, pay1, pay2, pay3, comp, posx, count, total):
    pays = (pay0, pay1, pay2, pay3)
    k64 = scal[6].astype(F32)
    mine, own = [], []
    for part in range(4):
        ctrl = pays[part][...].astype(F32)[72:80]
        local = ctrl[7:8] - k64
        live = ctrl[0:1] > 0.0
        mine.append(jnp.where(live & (local >= -1.0) & (local <= 63.0), 1.0, 0.0))
        own.append(jnp.where(live & (local >= 0.0) & (local <= 63.0), 1.0, 0.0))
    mine = jnp.concatenate([m[:, 128 * c : 128 * c + 128] for m in mine for c in range(8)], axis=0)
    own = jnp.concatenate([m[:, 128 * c : 128 * c + 128] for m in own for c in range(8)], axis=0)
    row = lax.broadcasted_iota(jnp.int32, (128, 128), 0)
    col = lax.broadcasted_iota(jnp.int32, (128, 128), 1)
    before = nn(mine.astype(BF), jnp.where(row < col, 1.0, 0.0).astype(BF))
    sums = nn(mine.astype(BF), jnp.ones((128, 128), BF))
    row4 = lax.broadcasted_iota(jnp.int32, (32, 32), 0)
    col4 = lax.broadcasted_iota(jnp.int32, (32, 32), 1)
    offset = nn(jnp.where(col4 < row4, 1.0, 0.0).astype(BF), sums.astype(BF))
    place = before + offset
    owned = jnp.where(own > 0.0, place, -1.0)
    posx[...] = owned
    total[...] = jnp.where(mine > 0.0, place, -1.0)
    number = jnp.sum(mine).astype(jnp.int32)
    count[0] = number
    comp[...] = jnp.zeros_like(comp)
    index = lax.broadcasted_iota(jnp.int32, (256, 128), 0).astype(F32)

    @pl.loop(0, (number + 255) // 256)
    def _(tile):
        ids = index + (tile * 256).astype(F32)
        out = jnp.zeros((80, 256), F32)
        for c in range(0, 32, 2):
            picks = jnp.concatenate(
                [jnp.where(ids == total[c + h : c + h + 1, :], 1.0, 0.0).astype(BF) for h in (0, 1)], axis=1
            )
            out = out + nt(pays[c // 8][:, 128 * (c % 8) : 128 * (c % 8) + 256], picks)
        comp[:, pl.ds(pl.multiple_of(tile * 256, 256), 256)] = out.astype(BF)


def expand_kernel(count, posx, found, *refs):
    outs, total = refs[0:4], refs[4]
    index = lax.broadcasted_iota(jnp.int32, (256, 128), 0).astype(F32)
    total[...] = jnp.zeros_like(total)

    @pl.loop(0, (count[0] + 255) // 256)
    def _(tile):
        ids = index + (tile * 256).astype(F32)
        rows = found[:, pl.ds(pl.multiple_of(tile * 256, 256), 256)]
        for c in range(32):
            picks = jnp.where(ids == posx[c : c + 1, :], 1.0, 0.0).astype(BF)
            total[:, 128 * c : 128 * c + 128] += nn(rows, picks)

    for m in range(4):
        outs[m][...] = total[:, 1024 * m : 1024 * m + 1024].astype(BF)


def convolve(act, weight, d, first, count, store):
    def part(i, dd, blocks):
        step = 2 * blocks * dd
        x = act[pl.ds(i - dd, step + 2 * dd)].reshape(blocks + 1, 2, dd, 96, 384)
        x = [x[p // 2 : p // 2 + blocks, p % 2].reshape(blocks * dd * 96, 384) for p in range(4)]
        y = nn(jnp.concatenate(x, axis=1), weight[...])
        y = jnp.stack([y[:, 128 * p : 128 * p + 128].reshape(blocks, dd, 96, 128) for p in (0, 1)], axis=1)
        store(pl.ds(i, step), y.reshape(step, 96, 128))

    for dd in range(1, 5):
        blocks = 8 // dd
        step = 2 * blocks * dd

        @pl.when(d == dd)
        def _():
            whole = (count + step // 2 - 1) // step

            @pl.loop(0, whole)
            def _(c):
                part(first + step * c, dd, blocks)

            @pl.when(count > whole * step)
            def _():
                part(first + step * whole, dd, blocks // 2)


def iterate(second, *refs):
    scal, count = refs[0:2]
    chunks = refs[2:6]
    enc_eye, dec_eye, dec_n, wf, wb, comp = refs[6:12]
    refs = refs[12:]
    if second:
        tots, from_prev, from_next = refs[0:2], refs[2], refs[3]
        outs, found = refs[4:8], refs[8]
        refs = refs[9:]
    else:
        outs = refs[0:2]
        refs = refs[2:]
    st, h, act, slope, bk, fct, wobs, g, ga, shift = refs

    act[60:96] = jnp.zeros((36, 96, 384), BF)

    for i in range(64):
        chunk = chunks[i // 16][i % 16]
        if 16 <= i < 48:
            both = tn(chunk, enc_eye[...])
            st[i - 16] = both[16:112, 128:256]
        else:
            both = tn(chunk, enc_eye[:, 0:128])
        h[i + OFF] = both[:, 0:128]
    if second:
        for half in range(2):
            tot = tots[half]
            for c in range(2):
                row = 32 * half + 16 * c
                lanes = 1024 * half + 512 * c
                for sec in range(3):
                    add = tot[:, 1024 * sec + 512 * c : 1024 * sec + 512 * c + 512].astype(F32)
                    if sec == 0:
                        add = add + from_prev[:, lanes : lanes + 512].astype(F32)
                    if sec == 2:
                        add = add + from_next[:, lanes : lanes + 512].astype(F32)
                    both = tn(add.astype(BF), enc_eye[...]).reshape(16, 32, 256)
                    h[row + OFF : row + OFF + 16, 16 + 32 * sec : 48 + 32 * sec, :] -= STEP * both[:, :, 0:128]
                    if half + c == 1:
                        st[row - 16 : row, 32 * sec : 32 + 32 * sec, :] -= STEP * both[:, :, 128:256]
                        ga[row - 16 : row, 32 * sec : 32 * sec + 32, :] = 0.75 * both[:, :, 128:256]
            low = tn(from_prev[:, 2048 + 128 * half : 2176 + 128 * half], enc_eye[:, 0:128])
            high = tn(from_next[:, 2048 + 128 * half : 2176 + 128 * half], enc_eye[:, 0:128])
            for i in range(32):
                h[32 * half + i + OFF, 15:16, :] -= STEP * low[32 + i : 33 + i]
                h[32 * half + i + OFF, 112:113, :] -= STEP * high[i : i + 1]

    e = lax.broadcasted_iota(jnp.int32, (112, 128), 0) + 8
    mask = jnp.where((e >= scal[4]) & (e < scal[5]), 1.0, 0.0)

    @pl.loop(0, 4)
    def _(l):
        d, reach = scal[l], reach_after(scal, l)
        first = 16 - reach - d + OFF

        @pl.loop(0, 16 + reach + d)
        def _(q):
            for u in range(2):
                i = first + 2 * q + u
                t = jnp.tanh(h[i, 8:120, :])
                slope[l, i] = ((1.0 - t * t) * mask)[8:104].astype(BF)
                t = t * mask
                shift[u] = t
                act[i, :, 0:128] = shift[u, pl.ds(8 - d, 96), :].astype(BF)
                act[i, :, 128:256] = t[8:104].astype(BF)
                act[i, :, 256:384] = shift[u, pl.ds(8 + d, 96), :].astype(BF)

        for u in range(R):
            slope[l, 48 + reach + d + OFF + u] = jnp.zeros((96, 128), BF)

        def store(rows, y):
            h[rows, 16:112, :] += y

        convolve(act, wf.at[l], d, 16 - reach + OFF, 32 + 2 * reach, store)

    for c in range(4):
        a = h[16 + OFF + 8 * c : 24 + OFF + 8 * c, 16:112, :].reshape(768, 128).astype(BF)
        b = st[8 * c : 8 + 8 * c].reshape(768, 128).astype(BF)
        fct[:, 768 * c : 768 * c + 768] = nt(dec_eye[...], jnp.concatenate([a, b], axis=1)).astype(BF)

    g[...] = jnp.zeros_like(g)
    k64 = scal[6].astype(F32)
    lon_of = lax.broadcasted_iota(jnp.int32, (32, 256), 0).astype(F32)
    lat_of = lax.broadcasted_iota(jnp.int32, (96, 256), 0).astype(F32) - 16.0

    @pl.loop(0, (count[0] + 255) // 256)
    def _(tile):
        lanes = pl.ds(pl.multiple_of(tile * 256, 256), 256)
        pay = comp[:, lanes].astype(F32)
        prec = pay[72:73] + pay[73:74]
        fu = pay[74:75] + pay[75:76]
        fv = pay[76:77] + pay[77:78]
        li, lj = pay[78:79], pay[79:80] - k64
        wa = jnp.where(lon_of == li, 1.0 - fu, 0.0) + jnp.where(lon_of == li + 1.0, fu, 0.0)
        wl = (jnp.where(lat_of == lj, 1.0 - fv, 0.0) + jnp.where(lat_of == lj + 1.0, fv, 0.0)).astype(BF)
        wa = wa.astype(BF)
        for i in range(32):
            wobs[96 * i : 96 * i + 96, :] = wa[i : i + 1] * wl
        eq = nn(fct[...], wobs[...])
        if second:
            found[:, lanes] = eq.astype(BF)
        wt = (prec * (eq - pay[0:72])).astype(BF)
        wt = jnp.concatenate([wt, jnp.zeros((56, 256), BF)], axis=0)
        for c in range(4):
            g[pl.ds(8 * c, 8)] += nt(wobs[768 * c : 768 * c + 768, :], wt).reshape(8, 96, 128)

    g[:, 0:16, :] = jnp.zeros((32, 16, 128), F32)
    g[:, 80:96, :] = jnp.zeros((32, 16, 128), F32)

    bk[...] = jnp.zeros_like(bk)
    act[0:24] = jnp.zeros((24, 96, 384), BF)
    act[56:96] = jnp.zeros((40, 96, 384), BF)
    for c in range(4):
        x = g[8 * c : 8 * c + 8].reshape(768, 128).astype(BF)
        bk[16 + OFF + 8 * c : 24 + OFF + 8 * c, 8:104, :] = nn(x, dec_n[...]).reshape(8, 96, 128)

    @pl.loop(0, 4)
    def _(back):
        l = 3 - back
        d, reach = scal[l], reach_after(scal, l)
        first = 16 - reach + OFF

        @pl.loop(0, 16 + reach)
        def _(q):
            for u in range(2):
                i = first + 2 * q + u
                act[i, :, 0:128] = bk[i, pl.ds(8 - d, 96), :].astype(BF)
                act[i, :, 128:256] = bk[i, 8:104, :].astype(BF)
                act[i, :, 256:384] = bk[i, pl.ds(8 + d, 96), :].astype(BF)

        def store(rows, y):
            bk[rows, 8:104, :] += slope[l, rows].astype(F32) * y

        convolve(act, wb.at[l], d, first - d, 32 + 2 * (reach + d), store)

    if second:
        ga[:, 0:16, :] = jnp.zeros((32, 16, 128), F32)
        ga[:, 80:96, :] = jnp.zeros((32, 16, 128), F32)
        edge = jnp.zeros((16, 128), BF)
        for i in range(64):
            x = jnp.concatenate([edge, bk[i + OFF, 8:104, :].astype(BF), edge], axis=0)
            if 16 <= i < 48:
                y = (g[i - 16] + ga[i - 16]).astype(BF)
                y = jnp.concatenate([edge, y, edge], axis=0)
                val = nt(enc_eye[...], jnp.concatenate([x, y], axis=1))
            else:
                val = nt(enc_eye[:, 0:128], x)
            outs[i // 16][i % 16] = (-STEP * val).astype(BF)
    else:
        for half in range(2):
            for c in range(2):
                lo = 32 * half + 16 * c
                for sec in range(3):
                    x = bk[lo + OFF : lo + OFF + 16, 32 * sec + 8 : 32 * sec + 40, :].reshape(512, 128).astype(BF)
                    if half + c == 1:
                        y = g[lo - 16 : lo, 32 * sec : 32 * sec + 32, :].reshape(512, 128).astype(BF)
                        val = nt(enc_eye[...], jnp.concatenate([x, y], axis=1))
                    else:
                        val = nt(enc_eye[:, 0:128], x)
                    outs[half][:, 1024 * sec + 512 * c : 1024 * sec + 512 * c + 512] = val.astype(BF)
            rows = []
            for col in (32, 63):
                for i in range(32):
                    x = bk[32 * half + i + OFF, col + 8 : col + 9, :]
                    here = 32 * half + i - 16
                    if 0 <= here < 32:
                        y = g[here, col : col + 1, :]
                    else:
                        y = jnp.zeros((1, 128), F32)
                    rows.append(jnp.concatenate([x, y], axis=1))
            rows.append(jnp.zeros((64, 256), F32))
            x = jnp.concatenate(rows, axis=0).astype(BF)
            outs[half][:, 3072:3200] = nt(enc_eye[...], x).astype(BF)


def iteration(second, scal, count, *arrays):
    smem = pl.BlockSpec(memory_space=pltpu.SMEM)
    vmem = pl.BlockSpec(memory_space=pltpu.VMEM)
    if second:
        shapes = [jax.ShapeDtypeStruct((16, V, 128), BF)] * 4 + [jax.ShapeDtypeStruct((V, 4096), BF)]
    else:
        shapes = [jax.ShapeDtypeStruct((V, 3200), BF)] * 2
    return pl.pallas_call(
        functools.partial(iterate, second),
        out_shape=shapes,
        in_specs=[smem, smem] + [vmem] * len(arrays),
        out_specs=[vmem] * len(shapes),
        scratch_shapes=[
            pltpu.VMEM((32, 96, 128), F32),
            pltpu.VMEM((ROWS, 128, 128), F32),
            pltpu.VMEM((ROWS, 96, 384), BF),
            pltpu.VMEM((4, ROWS, 96, 128), BF),
            pltpu.VMEM((ROWS, 112, 128), F32),
            pltpu.VMEM((V, 3072), BF),
            pltpu.VMEM((3072, 256), BF),
            pltpu.VMEM((32, 96, 128), F32),
            pltpu.VMEM((32, 96, 128), F32),
            pltpu.VMEM((2, 112, 128), F32),
        ],
        compiler_params=pltpu.CompilerParams(vmem_limit_bytes=VMEM),
        cost_estimate=pl.CostEstimate(flops=10**10, bytes_accessed=6 * 10**6, transcendentals=3 * 10**6),
        name="second_iteration" if second else "first_iteration",
    )(scal, count, *arrays)


def paired(taps):
    none = jnp.zeros((taps.shape[0], 384, 128), BF)
    low, mid, top = taps[:, 0], taps[:, 1], taps[:, 2]
    first = jnp.concatenate([low, mid, top, none], axis=1)
    later = jnp.concatenate([none, low, mid, top], axis=1)
    return jnp.concatenate([first, later], axis=2)


def make_weights(encoder_weight, convolution_weight, decoder_weight):
    eye = jnp.eye(V, 128, dtype=BF)
    enc_v = jnp.pad(encoder_weight.T, ((0, 128 - 69), (0, 0)))
    dec_v = jnp.pad(decoder_weight, ((0, 128 - 69), (0, 0)))
    ahead = convolution_weight.transpose(0, 1, 3, 2).reshape(4, 3, 384, 128)
    back = convolution_weight[:, ::-1].reshape(4, 3, 384, 128)
    return (
        jnp.concatenate([enc_v[0:V], eye], axis=1),
        jnp.concatenate([dec_v[0:V], eye], axis=1),
        dec_v,
        paired(ahead),
        paired(back),
    )


def on_device(
    background,
    encoder_weight,
    convolution_weight,
    decoder_weight,
    dilations,
    obs_values,
    obs_prec,
    obs_frac,
    obs_dest,
    obs_cell,
    obs_count,
):
    smem = pl.BlockSpec(memory_space=pltpu.SMEM)
    vmem = pl.BlockSpec(memory_space=pltpu.VMEM)
    lon, lat = lax.axis_index("lon"), lax.axis_index("lat")
    sub = lon % 4
    flip = lat % 2 == 1

    def block_of(s):
        return jnp.where(flip, 3 - s, s)

    place = lax.dynamic_slice(jnp.asarray(PLACES), (8 * lon + lat, 0), (1, 12)).reshape(12)
    scal = jnp.concatenate([dilations, place])

    cells = jnp.pad(background.astype(BF).transpose(1, 0, 2), ((0, 0), (0, V - 69), (0, 0)))
    before = lax.ppermute(cells[:, :, 224:256], AXES, BAND_UP)
    after = lax.ppermute(cells[:, :, 0:32], AXES, BAND_DOWN)
    sends = pl.pallas_call(
        split_kernel,
        out_shape=[jax.ShapeDtypeStruct((8, V, 128), BF)] * 4,
        in_specs=[smem] + [vmem] * 3,
        out_specs=[vmem] * 4,
        name="split",
    )(scal, cells, before, after)
    chunks = [sends[0]] + [lax.ppermute(sends[m], AXES, family(m)) for m in range(1, 4)]
    low, high = pl.pallas_call(
        order_kernel,
        out_shape=[jax.ShapeDtypeStruct((16, V, 128), BF)] * 2,
        in_specs=[smem] + [vmem] * 4,
        out_specs=[vmem] * 2,
        name="order",
    )(scal, *chunks)
    chunks = [lax.ppermute(high, AXES, LON_UP), low, high, lax.ppermute(low, AXES, LON_DOWN)]

    rows = obs_dest.shape[0]
    alive = (jnp.arange(rows, dtype=jnp.int32) < obs_count[0]).astype(F32)
    packed, slots = pl.pallas_call(
        pack_kernel,
        out_shape=[jax.ShapeDtypeStruct((80, 1024), BF), jax.ShapeDtypeStruct((1, rows), jnp.int32)],
        in_specs=[vmem] * 5,
        out_specs=[vmem] * 2,
        name="pack",
    )(obs_values, (alive * obs_prec)[None, :], obs_frac, obs_dest.reshape(1, rows), obs_cell[None, :])
    pick = (slots.reshape(rows, 1) == jnp.arange(1024, dtype=jnp.int32)[None, :]).astype(BF)
    arrived = lax.all_to_all(packed, AXES, split_axis=1, concat_axis=1, tiled=True, axis_index_groups=GROUPS_32)
    across = lax.ppermute(arrived, AXES, swap(2))
    others = [lax.ppermute(arrived, AXES, swap(1)), across, lax.ppermute(across, AXES, swap(1))]
    comp, posx, count = pl.pallas_call(
        compact_kernel,
        out_shape=[
            jax.ShapeDtypeStruct((80, 4096), BF),
            jax.ShapeDtypeStruct((32, 128), F32),
            jax.ShapeDtypeStruct((1,), jnp.int32),
        ],
        in_specs=[smem] + [vmem] * 4,
        out_specs=[vmem, vmem, smem],
        scratch_shapes=[pltpu.VMEM((32, 128), F32)],
        name="compact",
    )(scal, arrived, *others)

    weights = make_weights(encoder_weight, convolution_weight, decoder_weight)

    left, right = iteration(False, scal, count, *chunks, *weights, comp)
    left_in = lax.ppermute(right, AXES, LON_UP)
    right_in = lax.ppermute(left, AXES, LON_DOWN)
    left = (left.astype(F32) + left_in.astype(F32)).astype(BF)
    right = (right.astype(F32) + right_in.astype(F32)).astype(BF)
    extra = [left[:, 3072:3200], right[:, 3072:3200]]
    from_next = lax.ppermute(jnp.concatenate([left[:, 0:1024], right[:, 0:1024]] + extra, axis=1), AXES, LAT_DOWN)
    from_prev = lax.ppermute(jnp.concatenate([left[:, 2048:3072], right[:, 2048:3072]] + extra, axis=1), AXES, LAT_UP)
    *moves, found = iteration(True, scal, count, *chunks, *weights, comp, left, right, from_prev, from_next)

    low_in = lax.ppermute(moves[3], AXES, LON_UP)
    high_in = lax.ppermute(moves[0], AXES, LON_DOWN)

    spread = pl.pallas_call(
        expand_kernel,
        out_shape=[jax.ShapeDtypeStruct((V, 1024), BF)] * 4,
        in_specs=[smem, vmem, vmem],
        out_specs=[vmem] * 4,
        scratch_shapes=[pltpu.VMEM((V, 4096), F32)],
        name="expand",
    )(count, posx, found)
    parts = [lax.ppermute(spread[m], AXES, swap(m)) for m in range(1, 4)]
    parts = [p.astype(F32) for p in [spread[0]] + parts]
    spread = (parts[0] + parts[1] + parts[2] + parts[3]).astype(BF)
    spread = lax.all_to_all(spread, AXES, split_axis=1, concat_axis=1, tiled=True, axis_index_groups=GROUPS_32)
    equivalent = jnp.einsum("vs,rs->vr", spread[0:69], pick, preferred_element_type=F32)
    innovation = alive[None, :] * (equivalent - obs_values)

    moves = pl.pallas_call(
        gather_kernel,
        out_shape=[jax.ShapeDtypeStruct((8, V, 128), BF)] * 4,
        in_specs=[smem] + [vmem] * 4,
        out_specs=[vmem] * 4,
        name="gather",
    )(scal, moves[1], low_in, moves[2], high_in)
    back = [moves[0]] + [lax.ppermute(moves[m], AXES, [(b, a) for a, b in family(m)]) for m in range(1, 4)]
    total = jnp.zeros((8, V, 320), F32)
    summed = jnp.stack(back).astype(F32)
    for b in range(4):
        m = (jnp.where(flip, 3 - b, b) - sub) % 4
        block = lax.dynamic_index_in_dim(summed, m, 0, keepdims=False)
        total = total + jnp.pad(block, ((0, 0), (0, 0), (64 * b, 192 - 64 * b)))
    edge_up = lax.ppermute(total[:, :, 288:320].astype(BF), AXES, BAND_UP)
    edge_down = lax.ppermute(total[:, :, 0:32].astype(BF), AXES, BAND_DOWN)
    total = total[:, :, 32:288]
    total = total + jnp.pad(edge_up.astype(F32), ((0, 0), (0, 0), (0, 224)))
    total = total + jnp.pad(edge_down.astype(F32), ((0, 0), (0, 0), (224, 0)))
    analysis = background + total[:, 0:69, :].transpose(1, 0, 2)
    return (analysis, innovation)


def solution(mesh):
    placed = (
        P(None, "lon", "lat"),
        P(),
        P(),
        P(),
        P(),
        P(None, ("lon", "lat")),
        P(("lon", "lat")),
        P(None, ("lon", "lat")),
        P(("lon", "lat"), None),
        P(("lon", "lat")),
        P(("lon", "lat")),
    )
    return jax.shard_map(
        on_device,
        mesh=mesh,
        in_specs=placed,
        out_specs=(P(None, "lon", "lat"), P(None, ("lon", "lat"))),
        check_vma=False,
    )
```

```python
import functools

import jax
import jax.numpy as jnp
import numpy as np
from jax import lax
from jax.experimental import pallas as pl
from jax.experimental.pallas import tpu as pltpu
from jax.sharding import PartitionSpec as P

AXES = ("lon", "lat")
BF = jnp.bfloat16
F32 = jnp.float32
V = 72
OFF = 8
ROWS = 96
R = 16
STEP = 0.25
VMEM = 60 * 1024 * 1024


def snake(s, lat):
    return s if lat % 2 == 0 else 3 - s


def device(lon, lat):
    return 8 * lon + lat


def worker(y, p):
    lat, k = p // 4, p % 4
    return device(4 * y + snake(k, lat), lat)


LON_UP = [(worker(y, p), worker((y + 1) % 4, p)) for y in range(4) for p in range(32)]
LON_DOWN = [(b, a) for a, b in LON_UP]
LAT_UP = [(worker(y, p), worker(y, p + 1)) for y in range(4) for p in range(31)]
LAT_DOWN = [(b, a) for a, b in LAT_UP]
BAND_UP = [(device(n, l), device(n, l + 1)) for n in range(16) for l in range(7)]
BAND_DOWN = [(b, a) for a, b in BAND_UP]
GROUPS_32 = [[device(4 * y + s, l) for y in range(4) for l in range(8)] for s in range(4)]
GROUPS_4 = [[device(4 * y + s, l) for s in range(4)] for y in range(4) for l in range(8)]


def family(m):
    return [(g[s], g[(s + m) % 4]) for g in GROUPS_4 for s in range(4)]


def places():
    table = np.zeros((128, 12), np.int32)
    for n in range(16):
        for l in range(8):
            k = snake(n % 4, l)
            top = 256 * l + 64 * k
            table[8 * n + l, 0:3] = (32 - top, 2048 + 32 - top, 64 * k)
            for m in range(4):
                table[8 * n + l, 4 + m] = (n % 4 - m) % 4
                table[8 * n + l, 8 + m] = snake((n % 4 + m) % 4, l)
    return table


PLACES = places()


def reach_after(scal, l):
    return sum(jnp.where(l < n, scal[n], 0) for n in (1, 2, 3))


def swap(x):
    return [(g[s], g[s ^ x]) for g in GROUPS_4 for s in range(4)]


def nt(a, b):
    return lax.dot_general(a, b, (((1,), (1,)), ((), ())), preferred_element_type=F32)


def tn(a, b):
    return lax.dot_general(a, b, (((0,), (0,)), ((), ())), preferred_element_type=F32)


def nn(a, b):
    return jnp.dot(a, b, preferred_element_type=F32)


def pack_kernel(values, prec, frac, dest, cell, packed, slots):
    rows = dest.shape[1]
    owner = dest[...]
    group = lax.shift_right_logical(owner, 5) * 8 + (owner & 7)
    member = lax.broadcasted_iota(jnp.int32, (32, rows), 0) == group
    row = lax.broadcasted_iota(jnp.int32, (rows, rows), 0)
    col = lax.broadcasted_iota(jnp.int32, (rows, rows), 1)
    before = nn(jnp.where(member, 1.0, 0.0).astype(BF), jnp.where(row < col, 1.0, 0.0).astype(BF))
    rank = jnp.sum(jnp.where(member, before, 0.0), axis=0, keepdims=True)
    slot = group * 32 + rank.astype(jnp.int32)
    slots[...] = slot
    lon = jnp.zeros((1, rows), F32)
    code = cell[...]
    for step in range(1, 7):
        lon = lon + jnp.where(code >= 255 * step, 1.0, 0.0)
    lat = code.astype(F32) - 255.0 * lon
    lon = lon + 8.0 * (lax.shift_right_logical(owner, 3) & 3).astype(F32)
    parts = []
    for x in (prec[...], frac[0:1], frac[1:2]):
        high = x.astype(BF).astype(F32)
        parts += [high, x - high]
    ctrl = jnp.concatenate(parts + [lon, lat], axis=0)
    payload = jnp.concatenate([values[...], jnp.zeros((3, rows), F32), ctrl], axis=0).astype(BF)
    for c in range(4):
        index = lax.broadcasted_iota(jnp.int32, (256, rows), 0) + 256 * c
        pick = jnp.where(index == slot, 1.0, 0.0).astype(BF)
        packed[:, 256 * c : 256 * c + 256] = nt(payload, pick).astype(BF)


def split_kernel(scal, cells, before, after, *outs):
    for b in range(4):
        for m in range(4):
            @pl.when(scal[12 + m] == b)
            def _():
                for r in range(8):
                    if b == 0:
                        x = jnp.concatenate([before[r], cells[r, :, 0:96]], axis=1)
                    elif b == 3:
                        x = jnp.concatenate([cells[r, :, 160:256], after[r]], axis=1)
                    else:
                        x = cells[r, :, 64 * b - 32 : 64 * b + 96]
                    outs[m][r] = x


def order_kernel(scal, *refs):
    chunks, outs = refs[0:4], refs[4:6]
    for m in range(4):
        for c in range(4):
            @pl.when(scal[8 + m] == c)
            def _():
                outs[c // 2][8 * (c % 2) : 8 * (c % 2) + 8] = chunks[m][...]


def gather_kernel(scal, low, low_in, high, high_in, *outs):
    for m in range(4):
        for c in range(4):
            @pl.when(scal[8 + m] == c)
            def _():
                rows = pl.ds(8 * (c % 2), 8)
                x, y = (low, low_in) if c < 2 else (high, high_in)
                outs[m][...] = (x[rows].astype(F32) + y[rows].astype(F32)).astype(BF)


def compact_kernel(scal, pay0, pay1, pay2, pay3, comp, posx, count, total):
    pays = (pay0, pay1, pay2, pay3)
    k64 = scal[6].astype(F32)
    mine, own = [], []
    for part in range(4):
        ctrl = pays[part][...].astype(F32)[72:80]
        local = ctrl[7:8] - k64
        live = ctrl[0:1] > 0.0
        mine.append(jnp.where(live & (local >= -1.0) & (local <= 63.0), 1.0, 0.0))
        own.append(jnp.where(live & (local >= 0.0) & (local <= 63.0), 1.0, 0.0))
    mine = jnp.concatenate([m[:, 128 * c : 128 * c + 128] for m in mine for c in range(8)], axis=0)
    own = jnp.concatenate([m[:, 128 * c : 128 * c + 128] for m in own for c in range(8)], axis=0)
    row = lax.broadcasted_iota(jnp.int32, (128, 128), 0)
    col = lax.broadcasted_iota(jnp.int32, (128, 128), 1)
    before = nn(mine.astype(BF), jnp.where(row < col, 1.0, 0.0).astype(BF))
    sums = nn(mine.astype(BF), jnp.ones((128, 128), BF))
    row4 = lax.broadcasted_iota(jnp.int32, (32, 32), 0)
    col4 = lax.broadcasted_iota(jnp.int32, (32, 32), 1)
    offset = nn(jnp.where(col4 < row4, 1.0, 0.0).astype(BF), sums.astype(BF))
    place = before + offset
    owned = jnp.where(own > 0.0, place, -1.0)
    posx[...] = owned
    total[...] = jnp.where(mine > 0.0, place, -1.0)
    number = jnp.sum(mine).astype(jnp.int32)
    count[0] = number
    comp[...] = jnp.zeros_like(comp)
    index = lax.broadcasted_iota(jnp.int32, (256, 128), 0).astype(F32)

    @pl.loop(0, (number + 255) // 256)
    def _(tile):
        ids = index + (tile * 256).astype(F32)
        out = jnp.zeros((80, 256), F32)
        for c in range(0, 32, 2):
            picks = jnp.concatenate(
                [jnp.where(ids == total[c + h : c + h + 1, :], 1.0, 0.0).astype(BF) for h in (0, 1)], axis=1
            )
            out = out + nt(pays[c // 8][:, 128 * (c % 8) : 128 * (c % 8) + 256], picks)
        comp[:, pl.ds(pl.multiple_of(tile * 256, 256), 256)] = out.astype(BF)


def expand_kernel(count, posx, found, *refs):
    outs, total = refs[0:4], refs[4]
    index = lax.broadcasted_iota(jnp.int32, (256, 128), 0).astype(F32)
    total[...] = jnp.zeros_like(total)

    @pl.loop(0, (count[0] + 255) // 256)
    def _(tile):
        ids = index + (tile * 256).astype(F32)
        rows = found[:, pl.ds(pl.multiple_of(tile * 256, 256), 256)]
        for c in range(32):
            picks = jnp.where(ids == posx[c : c + 1, :], 1.0, 0.0).astype(BF)
            total[:, 128 * c : 128 * c + 128] += nn(rows, picks)

    for m in range(4):
        outs[m][...] = total[:, 1024 * m : 1024 * m + 1024].astype(BF)


def convolve(act, weight, d, first, count, store):
    def part(i, dd, blocks):
        step = 2 * blocks * dd
        x = act[pl.ds(i - dd, step + 2 * dd)].reshape(blocks + 1, 2, dd, 96, 384)
        x = [x[p // 2 : p // 2 + blocks, p % 2].reshape(blocks * dd * 96, 384) for p in range(4)]
        y = nn(jnp.concatenate(x, axis=1), weight[...])
        y = jnp.stack([y[:, 128 * p : 128 * p + 128].reshape(blocks, dd, 96, 128) for p in (0, 1)], axis=1)
        store(pl.ds(i, step), y.reshape(step, 96, 128))

    for dd in range(1, 5):
        blocks = 8 // dd
        step = 2 * blocks * dd

        @pl.when(d == dd)
        def _():
            whole = (count + step // 2 - 1) // step

            @pl.loop(0, whole // 2)
            def _(c):
                part(first + 2 * step * c, dd, blocks)
                part(first + 2 * step * c + step, dd, blocks)

            @pl.when(whole % 2 == 1)
            def _():
                part(first + step * (whole - 1), dd, blocks)

            @pl.when(count > whole * step)
            def _():
                part(first + step * whole, dd, blocks // 2)


def iterate(second, *refs):
    scal, count = refs[0:2]
    chunks = refs[2:6]
    enc_eye, dec_eye, dec_n, wf, wb, comp = refs[6:12]
    refs = refs[12:]
    if second:
        tots, from_prev, from_next = refs[0:2], refs[2], refs[3]
        outs, found = refs[4:8], refs[8]
        refs = refs[9:]
    else:
        outs = refs[0:2]
        refs = refs[2:]
    st, h, act, slope, bk, fct, wobs, g, ga, shift = refs

    act[60:96] = jnp.zeros((36, 96, 384), BF)

    for i in range(64):
        chunk = chunks[i // 16][i % 16]
        if 16 <= i < 48:
            both = tn(chunk, enc_eye[...])
            st[i - 16] = both[16:112, 128:256]
        else:
            both = tn(chunk, enc_eye[:, 0:128])
        h[i + OFF] = both[:, 0:128]
    if second:
        for half in range(2):
            tot = tots[half]
            for c in range(2):
                row = 32 * half + 16 * c
                lanes = 1024 * half + 512 * c
                for sec in range(3):
                    add = tot[:, 1024 * sec + 512 * c : 1024 * sec + 512 * c + 512].astype(F32)
                    if sec == 0:
                        add = add + from_prev[:, lanes : lanes + 512].astype(F32)
                    if sec == 2:
                        add = add + from_next[:, lanes : lanes + 512].astype(F32)
                    both = tn(add.astype(BF), enc_eye[...]).reshape(16, 32, 256)
                    h[row + OFF : row + OFF + 16, 16 + 32 * sec : 48 + 32 * sec, :] -= STEP * both[:, :, 0:128]
                    if half + c == 1:
                        st[row - 16 : row, 32 * sec : 32 + 32 * sec, :] -= STEP * both[:, :, 128:256]
                        ga[row - 16 : row, 32 * sec : 32 * sec + 32, :] = 0.75 * both[:, :, 128:256]
            low = tn(from_prev[:, 2048 + 128 * half : 2176 + 128 * half], enc_eye[:, 0:128])
            high = tn(from_next[:, 2048 + 128 * half : 2176 + 128 * half], enc_eye[:, 0:128])
            for i in range(32):
                h[32 * half + i + OFF, 15:16, :] -= STEP * low[32 + i : 33 + i]
                h[32 * half + i + OFF, 112:113, :] -= STEP * high[i : i + 1]

    e = lax.broadcasted_iota(jnp.int32, (112, 128), 0) + 8
    mask = jnp.where((e >= scal[4]) & (e < scal[5]), 1.0, 0.0)

    @pl.loop(0, 4)
    def _(l):
        d, reach = scal[l], reach_after(scal, l)
        first = 16 - reach - d + OFF

        @pl.loop(0, 16 + reach + d)
        def _(q):
            for u in range(2):
                i = first + 2 * q + u
                t = jnp.tanh(h[i, 8:120, :])
                slope[l, i] = ((1.0 - t * t) * mask)[8:104].astype(BF)
                t = t * mask
                shift[u] = t
                act[i, :, 0:128] = shift[u, pl.ds(8 - d, 96), :].astype(BF)
                act[i, :, 128:256] = t[8:104].astype(BF)
                act[i, :, 256:384] = shift[u, pl.ds(8 + d, 96), :].astype(BF)

        for u in range(R):
            slope[l, 48 + reach + d + OFF + u] = jnp.zeros((96, 128), BF)

        def store(rows, y):
            h[rows, 16:112, :] += y

        convolve(act, wf.at[l], d, 16 - reach + OFF, 32 + 2 * reach, store)

    for c in range(4):
        a = h[16 + OFF + 8 * c : 24 + OFF + 8 * c, 16:112, :].reshape(768, 128).astype(BF)
        b = st[8 * c : 8 + 8 * c].reshape(768, 128).astype(BF)
        fct[:, 768 * c : 768 * c + 768] = nt(dec_eye[...], jnp.concatenate([a, b], axis=1)).astype(BF)

    g[...] = jnp.zeros_like(g)
    k64 = scal[6].astype(F32)
    lon_of = lax.broadcasted_iota(jnp.int32, (32, 256), 0).astype(F32)
    lat_of = lax.broadcasted_iota(jnp.int32, (96, 256), 0).astype(F32) - 16.0

    @pl.loop(0, (count[0] + 255) // 256)
    def _(tile):
        lanes = pl.ds(pl.multiple_of(tile * 256, 256), 256)
        pay = comp[:, lanes].astype(F32)
        prec = pay[72:73] + pay[73:74]
        fu = pay[74:75] + pay[75:76]
        fv = pay[76:77] + pay[77:78]
        li, lj = pay[78:79], pay[79:80] - k64
        wa = jnp.where(lon_of == li, 1.0 - fu, 0.0) + jnp.where(lon_of == li + 1.0, fu, 0.0)
        wl = (jnp.where(lat_of == lj, 1.0 - fv, 0.0) + jnp.where(lat_of == lj + 1.0, fv, 0.0)).astype(BF)
        wa = wa.astype(BF)
        for i in range(32):
            wobs[96 * i : 96 * i + 96, :] = wa[i : i + 1] * wl
        eq = nn(fct[...], wobs[...])
        if second:
            found[:, lanes] = eq.astype(BF)
        wt = (prec * (eq - pay[0:72])).astype(BF)
        wt = jnp.concatenate([wt, jnp.zeros((56, 256), BF)], axis=0)
        for c in range(4):
            g[pl.ds(8 * c, 8)] += nt(wobs[768 * c : 768 * c + 768, :], wt).reshape(8, 96, 128)

    g[:, 0:16, :] = jnp.zeros((32, 16, 128), F32)
    g[:, 80:96, :] = jnp.zeros((32, 16, 128), F32)

    bk[...] = jnp.zeros_like(bk)
    act[0:24] = jnp.zeros((24, 96, 384), BF)
    act[56:96] = jnp.zeros((40, 96, 384), BF)
    for c in range(4):
        x = g[8 * c : 8 * c + 8].reshape(768, 128).astype(BF)
        bk[16 + OFF + 8 * c : 24 + OFF + 8 * c, 8:104, :] = nn(x, dec_n[...]).reshape(8, 96, 128)

    @pl.loop(0, 4)
    def _(back):
        l = 3 - back
        d, reach = scal[l], reach_after(scal, l)
        first = 16 - reach + OFF

        @pl.loop(0, 16 + reach)
        def _(q):
            for u in range(2):
                i = first + 2 * q + u
                act[i, :, 0:128] = bk[i, pl.ds(8 - d, 96), :].astype(BF)
                act[i, :, 128:256] = bk[i, 8:104, :].astype(BF)
                act[i, :, 256:384] = bk[i, pl.ds(8 + d, 96), :].astype(BF)

        def store(rows, y):
            bk[rows, 8:104, :] += slope[l, rows].astype(F32) * y

        convolve(act, wb.at[l], d, first - d, 32 + 2 * (reach + d), store)

    if second:
        ga[:, 0:16, :] = jnp.zeros((32, 16, 128), F32)
        ga[:, 80:96, :] = jnp.zeros((32, 16, 128), F32)
        edge = jnp.zeros((16, 128), BF)
        for i in range(64):
            x = jnp.concatenate([edge, bk[i + OFF, 8:104, :].astype(BF), edge], axis=0)
            if 16 <= i < 48:
                y = (g[i - 16] + ga[i - 16]).astype(BF)
                y = jnp.concatenate([edge, y, edge], axis=0)
                val = nt(enc_eye[...], jnp.concatenate([x, y], axis=1))
            else:
                val = nt(enc_eye[:, 0:128], x)
            outs[i // 16][i % 16] = (-STEP * val).astype(BF)
    else:
        for half in range(2):
            for c in range(2):
                lo = 32 * half + 16 * c
                for sec in range(3):
                    x = bk[lo + OFF : lo + OFF + 16, 32 * sec + 8 : 32 * sec + 40, :].reshape(512, 128).astype(BF)
                    if half + c == 1:
                        y = g[lo - 16 : lo, 32 * sec : 32 * sec + 32, :].reshape(512, 128).astype(BF)
                        val = nt(enc_eye[...], jnp.concatenate([x, y], axis=1))
                    else:
                        val = nt(enc_eye[:, 0:128], x)
                    outs[half][:, 1024 * sec + 512 * c : 1024 * sec + 512 * c + 512] = val.astype(BF)
            rows = []
            for col in (32, 63):
                for i in range(32):
                    x = bk[32 * half + i + OFF, col + 8 : col + 9, :]
                    here = 32 * half + i - 16
                    if 0 <= here < 32:
                        y = g[here, col : col + 1, :]
                    else:
                        y = jnp.zeros((1, 128), F32)
                    rows.append(jnp.concatenate([x, y], axis=1))
            rows.append(jnp.zeros((64, 256), F32))
            x = jnp.concatenate(rows, axis=0).astype(BF)
            outs[half][:, 3072:3200] = nt(enc_eye[...], x).astype(BF)


def iteration(second, scal, count, *arrays):
    smem = pl.BlockSpec(memory_space=pltpu.SMEM)
    vmem = pl.BlockSpec(memory_space=pltpu.VMEM)
    if second:
        shapes = [jax.ShapeDtypeStruct((16, V, 128), BF)] * 4 + [jax.ShapeDtypeStruct((V, 4096), BF)]
    else:
        shapes = [jax.ShapeDtypeStruct((V, 3200), BF)] * 2
    return pl.pallas_call(
        functools.partial(iterate, second),
        out_shape=shapes,
        in_specs=[smem, smem] + [vmem] * len(arrays),
        out_specs=[vmem] * len(shapes),
        scratch_shapes=[
            pltpu.VMEM((32, 96, 128), F32),
            pltpu.VMEM((ROWS, 128, 128), F32),
            pltpu.VMEM((ROWS, 96, 384), BF),
            pltpu.VMEM((4, ROWS, 96, 128), BF),
            pltpu.VMEM((ROWS, 112, 128), F32),
            pltpu.VMEM((V, 3072), BF),
            pltpu.VMEM((3072, 256), BF),
            pltpu.VMEM((32, 96, 128), F32),
            pltpu.VMEM((32, 96, 128), F32),
            pltpu.VMEM((2, 112, 128), F32),
        ],
        compiler_params=pltpu.CompilerParams(vmem_limit_bytes=VMEM),
        cost_estimate=pl.CostEstimate(flops=10**10, bytes_accessed=6 * 10**6, transcendentals=3 * 10**6),
        name="second_iteration" if second else "first_iteration",
    )(scal, count, *arrays)


def paired(taps):
    none = jnp.zeros((taps.shape[0], 384, 128), BF)
    low, mid, top = taps[:, 0], taps[:, 1], taps[:, 2]
    first = jnp.concatenate([low, mid, top, none], axis=1)
    later = jnp.concatenate([none, low, mid, top], axis=1)
    return jnp.concatenate([first, later], axis=2)


def make_weights(encoder_weight, convolution_weight, decoder_weight):
    eye = jnp.eye(V, 128, dtype=BF)
    enc_v = jnp.pad(encoder_weight.T, ((0, 128 - 69), (0, 0)))
    dec_v = jnp.pad(decoder_weight, ((0, 128 - 69), (0, 0)))
    ahead = convolution_weight.transpose(0, 1, 3, 2).reshape(4, 3, 384, 128)
    back = convolution_weight[:, ::-1].reshape(4, 3, 384, 128)
    return (
        jnp.concatenate([enc_v[0:V], eye], axis=1),
        jnp.concatenate([dec_v[0:V], eye], axis=1),
        dec_v,
        paired(ahead),
        paired(back),
    )


def on_device(
    background,
    encoder_weight,
    convolution_weight,
    decoder_weight,
    dilations,
    obs_values,
    obs_prec,
    obs_frac,
    obs_dest,
    obs_cell,
    obs_count,
):
    smem = pl.BlockSpec(memory_space=pltpu.SMEM)
    vmem = pl.BlockSpec(memory_space=pltpu.VMEM)
    lon, lat = lax.axis_index("lon"), lax.axis_index("lat")
    sub = lon % 4
    flip = lat % 2 == 1

    def block_of(s):
        return jnp.where(flip, 3 - s, s)

    place = lax.dynamic_slice(jnp.asarray(PLACES), (8 * lon + lat, 0), (1, 12)).reshape(12)
    scal = jnp.concatenate([dilations, place])

    cells = jnp.pad(background.astype(BF).transpose(1, 0, 2), ((0, 0), (0, V - 69), (0, 0)))
    before = lax.ppermute(cells[:, :, 224:256], AXES, BAND_UP)
    after = lax.ppermute(cells[:, :, 0:32], AXES, BAND_DOWN)
    sends = pl.pallas_call(
        split_kernel,
        out_shape=[jax.ShapeDtypeStruct((8, V, 128), BF)] * 4,
        in_specs=[smem] + [vmem] * 3,
        out_specs=[vmem] * 4,
        name="split",
    )(scal, cells, before, after)
    chunks = [sends[0]] + [lax.ppermute(sends[m], AXES, family(m)) for m in range(1, 4)]
    low, high = pl.pallas_call(
        order_kernel,
        out_shape=[jax.ShapeDtypeStruct((16, V, 128), BF)] * 2,
        in_specs=[smem] + [vmem] * 4,
        out_specs=[vmem] * 2,
        name="order",
    )(scal, *chunks)
    chunks = [lax.ppermute(high, AXES, LON_UP), low, high, lax.ppermute(low, AXES, LON_DOWN)]

    rows = obs_dest.shape[0]
    alive = (jnp.arange(rows, dtype=jnp.int32) < obs_count[0]).astype(F32)
    packed, slots = pl.pallas_call(
        pack_kernel,
        out_shape=[jax.ShapeDtypeStruct((80, 1024), BF), jax.ShapeDtypeStruct((1, rows), jnp.int32)],
        in_specs=[vmem] * 5,
        out_specs=[vmem] * 2,
        name="pack",
    )(obs_values, (alive * obs_prec)[None, :], obs_frac, obs_dest.reshape(1, rows), obs_cell[None, :])
    pick = (slots.reshape(rows, 1) == jnp.arange(1024, dtype=jnp.int32)[None, :]).astype(BF)
    arrived = lax.all_to_all(packed, AXES, split_axis=1, concat_axis=1, tiled=True, axis_index_groups=GROUPS_32)
    across = lax.ppermute(arrived, AXES, swap(2))
    others = [lax.ppermute(arrived, AXES, swap(1)), across, lax.ppermute(across, AXES, swap(1))]
    comp, posx, count = pl.pallas_call(
        compact_kernel,
        out_shape=[
            jax.ShapeDtypeStruct((80, 4096), BF),
            jax.ShapeDtypeStruct((32, 128), F32),
            jax.ShapeDtypeStruct((1,), jnp.int32),
        ],
        in_specs=[smem] + [vmem] * 4,
        out_specs=[vmem, vmem, smem],
        scratch_shapes=[pltpu.VMEM((32, 128), F32)],
        name="compact",
    )(scal, arrived, *others)

    weights = make_weights(encoder_weight, convolution_weight, decoder_weight)

    left, right = iteration(False, scal, count, *chunks, *weights, comp)
    left_in = lax.ppermute(right, AXES, LON_UP)
    right_in = lax.ppermute(left, AXES, LON_DOWN)
    left = (left.astype(F32) + left_in.astype(F32)).astype(BF)
    right = (right.astype(F32) + right_in.astype(F32)).astype(BF)
    extra = [left[:, 3072:3200], right[:, 3072:3200]]
    from_next = lax.ppermute(jnp.concatenate([left[:, 0:1024], right[:, 0:1024]] + extra, axis=1), AXES, LAT_DOWN)
    from_prev = lax.ppermute(jnp.concatenate([left[:, 2048:3072], right[:, 2048:3072]] + extra, axis=1), AXES, LAT_UP)
    *moves, found = iteration(True, scal, count, *chunks, *weights, comp, left, right, from_prev, from_next)

    low_in = lax.ppermute(moves[3], AXES, LON_UP)
    high_in = lax.ppermute(moves[0], AXES, LON_DOWN)

    spread = pl.pallas_call(
        expand_kernel,
        out_shape=[jax.ShapeDtypeStruct((V, 1024), BF)] * 4,
        in_specs=[smem, vmem, vmem],
        out_specs=[vmem] * 4,
        scratch_shapes=[pltpu.VMEM((V, 4096), F32)],
        name="expand",
    )(count, posx, found)
    parts = [lax.ppermute(spread[m], AXES, swap(m)) for m in range(1, 4)]
    parts = [p.astype(F32) for p in [spread[0]] + parts]
    spread = (parts[0] + parts[1] + parts[2] + parts[3]).astype(BF)
    spread = lax.all_to_all(spread, AXES, split_axis=1, concat_axis=1, tiled=True, axis_index_groups=GROUPS_32)
    equivalent = jnp.einsum("vs,rs->vr", spread[0:69], pick, preferred_element_type=F32)
    innovation = alive[None, :] * (equivalent - obs_values)

    moves = pl.pallas_call(
        gather_kernel,
        out_shape=[jax.ShapeDtypeStruct((8, V, 128), BF)] * 4,
        in_specs=[smem] + [vmem] * 4,
        out_specs=[vmem] * 4,
        name="gather",
    )(scal, moves[1], low_in, moves[2], high_in)
    back = [moves[0]] + [lax.ppermute(moves[m], AXES, [(b, a) for a, b in family(m)]) for m in range(1, 4)]
    total = jnp.zeros((8, V, 320), F32)
    summed = jnp.stack(back).astype(F32)
    for b in range(4):
        m = (jnp.where(flip, 3 - b, b) - sub) % 4
        block = lax.dynamic_index_in_dim(summed, m, 0, keepdims=False)
        total = total + jnp.pad(block, ((0, 0), (0, 0), (64 * b, 192 - 64 * b)))
    edge_up = lax.ppermute(total[:, :, 288:320].astype(BF), AXES, BAND_UP)
    edge_down = lax.ppermute(total[:, :, 0:32].astype(BF), AXES, BAND_DOWN)
    total = total[:, :, 32:288]
    total = total + jnp.pad(edge_up.astype(F32), ((0, 0), (0, 0), (0, 224)))
    total = total + jnp.pad(edge_down.astype(F32), ((0, 0), (0, 0), (224, 0)))
    analysis = background + total[:, 0:69, :].transpose(1, 0, 2)
    return (analysis, innovation)


def solution(mesh):
    placed = (
        P(None, "lon", "lat"),
        P(),
        P(),
        P(),
        P(),
        P(None, ("lon", "lat")),
        P(("lon", "lat")),
        P(None, ("lon", "lat")),
        P(("lon", "lat"), None),
        P(("lon", "lat")),
        P(("lon", "lat")),
    )
    return jax.shard_map(
        on_device,
        mesh=mesh,
        in_specs=placed,
        out_specs=(P(None, "lon", "lat"), P(None, ("lon", "lat"))),
        check_vma=False,
    )
```
